256 devices in a mesh: row: 16 (over z_hi, x), col: 16 (over y, z_lo, core).
Axes of the slice: x: 4, y: 4, z: 8 (z_hi: 4, z_lo: 2; z = z_hi * 2 + z_lo), core: 2. Of those that a mesh axis runs over, the one named last changes fastest.
Arguments:
- matrix: bfloat16 [2, 4096, 40, 4096], P(None, 'row', None, 'col'), may hold values from -0.015625 to 0.015625
- diagonal: float32 [4096, 40], P(('col', 'row')), may hold values from 2.5 to 5
- right_side: float32 [4096, 40, 64], P(('col', 'row')), may hold values from -6 to 6
- slab_first: int32 [1], replicated, may hold values from 0 to 608
Outputs:
- solution: float32 [4096, 40, 64], P(('col', 'row'))
- residual: float32 [4096, 40, 64], P(('col', 'row'))
The draws below stay inside these ranges and needn't reach their ends.
All inputs are finite; a program needn't handle non-finite values.
Results may differ from the reference program's by a relative error of at most 0.04.
Values may be sent and summed in bfloat16 or wider, within the bound.
A program may use at most 128 MiB of HBM per device.

```python
import math
import jax
import jax.numpy as jnp
from jax import lax

BS = 256
RB_DEV = 2
CB_DEV = 40
RHS = 64
ITERS = 3
NCB = 640
NRB = 32
ORDER = 163840
ROWSPAN = 4096
COLSPAN = 4096
N_ROW = 16
N_COL = 16


def level_of(rng, dims, pieces, smallest, top_value):
    loudness, own = 1.0, jax.random.fold_in(rng, 6)
    for axis_at, blocks in pieces:
        steps = jnp.exp(jax.random.uniform(jax.random.fold_in(own, axis_at), (blocks,), jnp.float32, smallest / len(pieces), top_value / len(pieces)))
        loudness = loudness * jnp.repeat(steps, dims[axis_at] // blocks).reshape([-1 if axis == axis_at else 1 for axis in range(len(dims))])
    return loudness


def gaussian(own_key, shape, scale, most, split=(), kind=jnp.bfloat16):
    values = scale * jax.random.normal(own_key, shape, jnp.float32)
    if split:
        values = values * level_of(own_key, shape, split, -0.22, 0.18)
    return jnp.clip(values, -most, most).astype(kind)


def setup_inputs(seed: int = 0) -> dict:
    key_list = jax.random.split(jax.random.key(seed), 5)
    return {
        "matrix": gaussian(key_list[0], (RB_DEV, ROWSPAN, CB_DEV, COLSPAN), ORDER ** -0.5, 0.015625, ((1, 16), (3, 16))),
        "diagonal": jnp.clip(jnp.exp(math.log(5.0) - 0.6931472 * jax.random.uniform(key_list[1], (COLSPAN, CB_DEV), jnp.float32) ** level_of(key_list[1], (COLSPAN, CB_DEV), ((0, 256),), -0.2, 0.2)), 2.5, 5.0),
        "right_side": gaussian(key_list[2], (COLSPAN, CB_DEV, RHS), 1.0, 6.0, ((0, 256),), jnp.float32),
        "slab_first": jax.random.randint(key_list[3], (1,), 0, NCB - NRB + 1).astype(jnp.int32),
    }


def reference(matrix, diagonal, right_side, slab_first):
    row_count = N_ROW
    col_count = N_COL
    block_rows = (jnp.arange(RB_DEV)[:, None] * row_count + jnp.arange(row_count)[None, :]).astype(jnp.int32)
    global_rows = (slab_first[0] + block_rows).reshape(-1).astype(jnp.int32)
    block_cols = (jnp.arange(CB_DEV)[:, None] * col_count + jnp.arange(col_count)[None, :]).astype(jnp.int32)
    lower = block_cols[None] < global_rows[:, None, None]
    onblock = block_cols[None] == global_rows[:, None, None]
    weights = jnp.where(lower, 1.0, jnp.where(onblock, 0.5, 0.0)).astype(jnp.float32)
    weights4 = weights.reshape(RB_DEV, row_count, CB_DEV, col_count)
    panels4 = matrix.reshape(RB_DEV, row_count, BS, CB_DEV * col_count * BS)
    home_col = (global_rows % col_count).astype(jnp.int32)
    home_blk = (global_rows // col_count).astype(jnp.int32)

    def operate(vector):
        grid = vector.astype(jnp.bfloat16).reshape(col_count, BS, CB_DEV, RHS)
        slab_direction = grid[home_col, :, home_blk, :]
        slab4 = slab_direction.reshape(RB_DEV, row_count, BS, RHS)
        by_block = jnp.transpose(grid, (2, 0, 1, 3))

        def visit(running, index_position):
            partial_value = jnp.zeros((RHS, CB_DEV, col_count, BS), jnp.float32)
            values = []
            for blk in range(RB_DEV):
                panel = panels4[blk, index_position]
                weight = weights4[blk, index_position]
                own = slab4[blk, index_position]
                masked = (weight[:, :, None, None].astype(jnp.bfloat16) * by_block).reshape(-1, RHS)
                values.append(jnp.dot(panel, masked, preferred_element_type=jnp.float32))
                mirror = jnp.dot(own.T, panel, preferred_element_type=jnp.float32)
                mirror = mirror.reshape(RHS, CB_DEV, col_count, BS)
                partial_value = partial_value + mirror * weight[None, :, :, None]
            return running + partial_value, jnp.stack(values)

        start = jnp.zeros((RHS, CB_DEV, col_count, BS), jnp.float32)
        mirrored, row_values = lax.scan(visit, start, jnp.arange(row_count, dtype=jnp.int32))
        row_values = jnp.transpose(row_values, (1, 0, 2, 3)).reshape(RB_DEV * row_count, BS, RHS)
        result = jnp.transpose(mirrored, (2, 3, 1, 0))
        result = result.at[home_col, :, home_blk, :].add(row_values)
        return diagonal[:, :, None] * vector + result.reshape(col_count * BS, CB_DEV, RHS)

    solution = jnp.zeros_like(right_side)
    residual = right_side
    direction = right_side
    norm_now = jnp.sum(residual * residual, axis=(0, 1))
    for step in range(ITERS):
        image = operate(direction)
        step_length = norm_now / jnp.sum(direction * image, axis=(0, 1))
        solution = solution + step_length * direction
        residual = residual - step_length * image
        norm_next = jnp.sum(residual * residual, axis=(0, 1))
        direction = residual + (norm_next / norm_now) * direction
        norm_now = norm_next
    return solution, residual
```

```python
import functools

import jax
import jax.numpy as jnp
from jax import lax
from jax.experimental import pallas as pl
from jax.experimental.pallas import tpu as pltpu
from jax.sharding import PartitionSpec as P

ITERS = 3
NX = 4
MESH = pl.DeviceIdType.MESH
F32 = jnp.float32
BF16 = jnp.bfloat16
LANES = 128
HALF = 64
CELLS = 16
MSG = CELLS + 8


def column_sums(values):
    total = jnp.sum(jnp.sum(values, axis=0), axis=0, keepdims=True)
    total = jnp.broadcast_to(total, (8, LANES))
    return total + pltpu.roll(total, HALF, 1)


def kernel(
    nx, nz,
    first_ref, matrix_hbm, diag_ref, right_ref,
    sol_ref, res_ref,
    matrix, gathered, mirror, got_x, sums_z, got_z,
    direction, image, slab_dir, slab_img, acc, norm_ref,
    out1, in1, out2, in2, out_a, in_a, out_b, in_b,
    load_sem, gz_send, gz_recv, gx_send, gx_recv,
    mx_send, mx_recv, mz_send, mz_recv, hop_send, hop_recv,
):
    n = nx * nz
    pairs = diag_ref.shape[0]
    order = n * CELLS
    i = lax.axis_index("row")
    j = lax.axis_index("col")
    z = i // nx
    x = i % nx
    first = first_ref[0]
    my_row = (j - first) & (n - 1)
    my_block = (first + my_row) // n
    my_col = (first + i) & (n - 1)
    odd = (my_block & 1) == 1

    load = pltpu.make_async_copy(matrix_hbm, matrix, load_sem)
    load.start()

    block_of = (
        2 * lax.broadcasted_iota(jnp.int32, (pairs, CELLS, LANES), 0)
        + lax.broadcasted_iota(jnp.int32, (pairs, CELLS, LANES), 2) // HALF
    )
    owned = (block_of == my_block) | (block_of == my_block + 1)
    slot_of = lax.broadcasted_iota(jnp.int32, (n, CELLS, LANES), 0)
    left_half = lax.broadcasted_iota(jnp.int32, (order, LANES), 1) < HALF
    even_lanes = (lax.broadcasted_iota(jnp.int32, (CELLS, LANES), 1) < HALF).astype(F32)
    even_mask = even_lanes.astype(BF16)
    odd_mask = (1.0 - even_lanes).astype(BF16)

    def swap(piece):
        return jnp.where(odd, pltpu.roll(piece, HALF, 1), piece)

    def row_copy(src, dst, send, recv, zz, xx):
        return pltpu.make_async_remote_copy(
            src_ref=src, dst_ref=dst, send_sem=send, recv_sem=recv,
            device_id=(zz * nx + xx, j), device_id_type=MESH,
        )

    def hop_copy(src, dst, k, h, row, col):
        return pltpu.make_async_remote_copy(
            src_ref=src, dst_ref=dst, send_sem=hop_send.at[k, h],
            recv_sem=hop_recv.at[k, h], device_id=(row, col), device_id_type=MESH,
        )

    sol_ref[...] = jnp.zeros_like(sol_ref)
    res_ref[...] = right_ref[...]
    direction[...] = jnp.zeros_like(direction)
    image[...] = jnp.zeros_like(image)
    slab_dir[...] = jnp.zeros_like(slab_dir)
    slab_img[...] = jnp.zeros_like(slab_img)
    norm_ref[...] = jnp.ones_like(norm_ref)

    def iteration(k, carry):
        residual = res_ref[...]
        gathered[k, z, x] = residual.astype(BF16)

        def spread_z(dz):
            return row_copy(
                gathered.at[k, z, x], gathered.at[k, z, x],
                gz_send.at[k, dz - 1], gz_recv.at[k, dz - 1], (z + dz) % nz, x,
            )

        def spread_x(dx, dz):
            zz = (z - dz + nz) % nz
            return row_copy(
                gathered.at[k, zz, x], gathered.at[k, zz, x],
                gx_send.at[k, dz, dx - 1], gx_recv.at[k, dz, dx - 1], z, (x + dx) % nx,
            )

        for dz in range(1, nz):
            spread_z(dz).start()

        piece = swap(jnp.sum(jnp.where(owned, residual, 0.0), axis=0))
        out1[k, 0:CELLS] = piece
        out1[k, CELLS:MSG] = column_sums(residual * residual)

        def hop1(step, c):
            row = (i + step) % n

            @pl.when((row != i) | (i != j))
            def _():
                hop_copy(out1.at[k], in1.at[k, j], k, 0, row, i).start()

            return c

        lax.fori_loop(0, n, hop1, 0)

        @pl.when(i == j)
        def _():
            in1[k, j] = out1[k]

        for dx in range(1, nx):
            spread_x(dx, 0).start()

        def hop_wait(buf, h, slots):
            hop_copy(buf.at[k, 0:slots], buf.at[k, 0:slots], k, h, i, j).wait()

        def wait_cross(buf, h):
            @pl.when(i == j)
            def _():
                hop_wait(buf, h, n - 1)

            @pl.when(i != j)
            def _():
                hop_wait(buf, h, n)

        wait_cross(in1, 0)
        piece = jnp.sum(jnp.where(slot_of == my_col, in1[k, :, 0:CELLS, :], 0.0), axis=0)
        sums = jnp.sum(in1[k, :, CELLS:MSG, :], axis=0)
        out2[k, 0:CELLS] = piece
        out2[k, CELLS:MSG] = sums
        in2[k, j] = out2[k]

        def hop2(step, c):
            hop_copy(out2.at[k], in2.at[k, j], k, 1, i, (j + step) % n).start()
            return c

        lax.fori_loop(1, n, hop2, 0)

        for dz in range(1, nz):
            spread_z(dz).wait()
            for dx in range(1, nx):
                spread_x(dx, dz).start()

        hop_wait(in2, 1, n - 1)
        slab = in2[k, :, 0:CELLS, :].reshape(order, LANES)
        norm = jnp.sum(in2[k, :, CELLS:MSG, :], axis=0)
        beta = jnp.where(k == 0, 0.0, norm / norm_ref[...])
        norm_ref[...] = norm
        beta_row = beta[0:1, :]
        slab_d = slab + beta_row * slab_dir[...]
        slab_dir[...] = slab_d
        beta_cell = beta_row.reshape(1, 1, LANES)
        cells_d = residual + beta_cell * direction[...]
        direction[...] = cells_d

        @pl.when(k == 0)
        def _():
            load.wait()

        turned = jnp.transpose(slab).astype(BF16)
        both = jnp.concatenate([turned[0:HALF], turned[HALF:LANES]], axis=1)

        def transposed(p, c):
            parts = [
                jnp.dot(both, matrix[2 * p + h], preferred_element_type=F32)
                for h in range(2)
            ]
            cells = jnp.transpose(jnp.concatenate(parts, axis=0))
            mirror[:, :, p] = cells.astype(BF16).reshape(nz, nx, CELLS, LANES)
            return c

        lax.fori_loop(0, pairs, transposed, 0)

        def mirror_x(dx):
            xx = (x + dx) % nx
            return row_copy(
                mirror.at[:, xx], got_x.at[k, dx - 1],
                mx_send.at[k, dx - 1], mx_recv.at[k, dx - 1], z, xx,
            )

        def mirror_z(dz):
            zz = (z + dz) % nz
            return row_copy(
                sums_z.at[zz], got_z.at[k, dz - 1],
                mz_send.at[k, dz - 1], mz_recv.at[k, dz - 1], zz, x,
            )

        for dx in range(1, nx):
            mirror_x(dx).start()

        for dz in range(nz):
            for dx in range(1, nx):
                spread_x(dx, dz).wait()

        acc[...] = jnp.zeros_like(acc)

        def forward(p, c):
            cells = gathered[k, :, :, p].reshape(n, CELLS, LANES)
            evens = (cells * even_mask).reshape(order, LANES)
            odds = (cells * odd_mask).reshape(order, LANES)
            acc[...] += jnp.dot(matrix[2 * p], evens, preferred_element_type=F32) + jnp.dot(
                matrix[2 * p + 1], odds, preferred_element_type=F32
            )
            return c

        lax.fori_loop(0, pairs, forward, 0)
        rows = acc[...]
        rows = rows + pltpu.roll(rows, HALF, 1)
        rows = jnp.where(left_half, rows[0:order], rows[order:])
        slab_q = rows + beta_row * slab_img[...]
        slab_img[...] = slab_q
        curve = column_sums(diag_ref[...] * cells_d * cells_d)
        curve = curve + 2.0 * column_sums((slab_d * slab_q).reshape(n, CELLS, LANES))

        out_a[k, :, 0:CELLS] = rows.reshape(n, CELLS, LANES)
        out_a[k, :, CELLS:MSG] = jnp.broadcast_to(curve, (n, 8, LANES))
        in_a[k, j] = out_a[k, j]

        def hop_a(step, c):
            col = (j + step) % n
            hop_copy(out_a.at[k, col], in_a.at[k, j], k, 2, i, col).start()
            return c

        lax.fori_loop(1, n, hop_a, 0)

        for dx in range(1, nx):
            mirror_x(dx).wait()
        for dz in range(nz):
            zz = (z + dz) % nz
            total = mirror[zz, x].astype(F32)
            for dx in range(1, nx):
                total = total + got_x[k, dx - 1, zz].astype(F32)
            sums_z[zz] = total.astype(BF16)
        for dz in range(1, nz):
            mirror_z(dz).start()

        hop_wait(in_a, 2, n - 1)
        out_b[k] = jnp.sum(in_a[k], axis=0)

        def hop_b(step, c):
            col = (j + step) % n

            @pl.when((col != j) | (i != j))
            def _():
                hop_copy(out_b.at[k], in_b.at[k, i], k, 3, j, col).start()

            return c

        lax.fori_loop(0, n, hop_b, 0)

        @pl.when(i == j)
        def _():
            in_b[k, i] = out_b[k]

        for dz in range(1, nz):
            mirror_z(dz).wait()
        applied = diag_ref[...] * residual + sums_z[z].astype(F32)
        for dz in range(1, nz):
            applied = applied + got_z[k, dz - 1].astype(F32)

        wait_cross(in_b, 3)
        piece = swap(
            jnp.sum(jnp.where(slot_of == my_row, in_b[k, :, 0:CELLS, :], 0.0), axis=0)
        )
        curve = jnp.sum(in_b[k, :, CELLS:MSG, :], axis=0)
        applied = applied + jnp.where(owned, piece.reshape(1, CELLS, LANES), 0.0)
        applied = applied + beta_cell * image[...]
        image[...] = applied
        length = (norm / curve)[0:1, :].reshape(1, 1, LANES)
        sol_ref[...] = sol_ref[...] + length * cells_d
        res_ref[...] = residual - length * applied
        return carry

    lax.fori_loop(0, ITERS, iteration, 0)


def body(nx, matrix, diagonal, right_side, slab_first):
    n = lax.axis_size("row")
    nz = n // nx
    rb, order, blocks, _ = matrix.shape
    cells, _, width = right_side.shape
    pairs = blocks // 2
    rows = slab_first[0] + jnp.arange(rb, dtype=jnp.int32) * n + lax.axis_index("row")
    cols = jnp.arange(blocks, dtype=jnp.int32) * n + lax.axis_index("col")
    weight = jnp.where(
        cols[:, None] < rows[None, :], 1.0, jnp.where(cols[:, None] == rows[None, :], 0.5, 0.0)
    ).astype(matrix.dtype)
    turned = jnp.transpose(matrix, (2, 0, 1, 3)) * weight[:, :, None, None]
    turned = turned.reshape(blocks, rb * order, order)

    def packed(cell_array):
        return jnp.transpose(cell_array.reshape(cells, pairs, LANES), (1, 0, 2))

    def unpacked(cell_array):
        return jnp.transpose(cell_array, (1, 0, 2)).reshape(cells, blocks, width)

    diag = packed(jnp.broadcast_to(diagonal[:, :, None], right_side.shape))
    vec = (pairs, cells, LANES)
    vmem = pl.BlockSpec(memory_space=pltpu.VMEM)
    dma = pltpu.SemaphoreType.DMA
    sol, res = pl.pallas_call(
        functools.partial(kernel, nx, nz),
        out_shape=[jax.ShapeDtypeStruct(vec, F32)] * 2,
        in_specs=[
            pl.BlockSpec(memory_space=pltpu.SMEM),
            pl.BlockSpec(memory_space=pl.ANY),
            vmem,
            vmem,
        ],
        out_specs=[vmem, vmem],
        scratch_shapes=[
            pltpu.VMEM((blocks, rb * order, order), BF16),
            pltpu.VMEM((ITERS, nz, nx) + vec, BF16),
            pltpu.VMEM((nz, nx) + vec, BF16),
            pltpu.VMEM((ITERS, nx - 1, nz) + vec, BF16),
            pltpu.VMEM((nz,) + vec, BF16),
            pltpu.VMEM((ITERS, nz - 1) + vec, BF16),
            pltpu.VMEM(vec, F32),
            pltpu.VMEM(vec, F32),
            pltpu.VMEM((order, LANES), F32),
            pltpu.VMEM((order, LANES), F32),
            pltpu.VMEM((rb * order, LANES), F32),
            pltpu.VMEM((8, LANES), F32),
            pltpu.VMEM((ITERS, MSG, LANES), F32),
            pltpu.VMEM((ITERS, n, MSG, LANES), F32),
            pltpu.VMEM((ITERS, MSG, LANES), F32),
            pltpu.VMEM((ITERS, n, MSG, LANES), F32),
            pltpu.VMEM((ITERS, n, MSG, LANES), F32),
            pltpu.VMEM((ITERS, n, MSG, LANES), F32),
            pltpu.VMEM((ITERS, MSG, LANES), F32),
            pltpu.VMEM((ITERS, n, MSG, LANES), F32),
            dma,
            dma((ITERS, nz - 1)),
            dma((ITERS, nz - 1)),
            dma((ITERS, nz, nx - 1)),
            dma((ITERS, nz, nx - 1)),
            dma((ITERS, nx - 1)),
            dma((ITERS, nx - 1)),
            dma((ITERS, nz - 1)),
            dma((ITERS, nz - 1)),
            dma((ITERS, 4)),
            dma((ITERS, 4)),
        ],
        compiler_params=pltpu.CompilerParams(
            has_side_effects=True, vmem_limit_bytes=48 * 1024 * 1024
        ),
        name="conjugate_gradients",
    )(slab_first, turned, diag, packed(right_side))
    return unpacked(sol), unpacked(res)


def solution(mesh, nx=NX):
    placed = (
        P(None, "row", None, "col"),
        P(("col", "row"), None),
        P(("col", "row"), None, None),
        P(),
    )
    return jax.shard_map(
        functools.partial(body, nx),
        mesh=mesh,
        in_specs=placed,
        out_specs=(P(("col", "row"), None, None), P(("col", "row"), None, None)),
        check_vma=False,
    )
```

```python
import functools

import jax
import jax.numpy as jnp
from jax import lax
from jax.experimental import pallas as pl
from jax.experimental.pallas import tpu as pltpu
from jax.sharding import PartitionSpec as P

ITERS = 3
NX = 4
CHUNKS = 4
ROWS = 32
MESH = pl.DeviceIdType.MESH
F32 = jnp.float32
BF16 = jnp.bfloat16
LANES = 128
HALF = 64
CELLS = 16


def column_sums(values):
    total = jnp.sum(jnp.sum(values, axis=0), axis=0, keepdims=True)
    return total + pltpu.roll(total, HALF, 1)


def kernel(
    nx, nz,
    first_ref, matrix_hbm, diag_ref, right_ref,
    sol_ref, res_ref,
    raw, matrix, gathered, mirror, got_x, sums_z, got_z,
    direction, image, slab_dir, slab_img,
    out1, in1, out2, in2, out_a, in_a, out_b, in_b, out_s, in_s,
    load_sem, gz_send, gz_recv, gx_send, gx_recv,
    mx_send, mx_recv, mz_send, mz_recv, hop_send, hop_recv,
):
    n = nx * nz
    pairs = diag_ref.shape[0]
    order = n * CELLS
    block_rows, _, blocks, _ = raw.shape
    per_chunk = pairs // CHUNKS
    turn_rows = min(ROWS, order)
    i = lax.axis_index("row")
    j = lax.axis_index("col")
    z = i // nx
    x = i % nx
    first = first_ref[0]
    my_row = (j - first) & (n - 1)
    my_block = (first + my_row) // n
    my_col = (first + i) & (n - 1)
    odd = (my_block & 1) == 1

    def load(a):
        return pltpu.make_async_copy(matrix_hbm.at[a], raw.at[a], load_sem.at[a])

    for a in range(block_rows):
        load(a).start()

    block_of = (
        2 * lax.broadcasted_iota(jnp.int32, (pairs, CELLS, LANES), 0)
        + lax.broadcasted_iota(jnp.int32, (pairs, CELLS, LANES), 2) // HALF
    )
    owned = (block_of == my_block) | (block_of == my_block + 1)
    slot_of = lax.broadcasted_iota(jnp.int32, (n, CELLS, LANES), 0)
    left_half = lax.broadcasted_iota(jnp.int32, (order, LANES), 1) < HALF
    even_lanes = (lax.broadcasted_iota(jnp.int32, (CELLS, LANES), 1) < HALF).astype(F32)
    even_mask = even_lanes.astype(BF16)
    odd_mask = (1.0 - even_lanes).astype(BF16)

    def swap(piece):
        return jnp.where(odd, pltpu.roll(piece, HALF, 1), piece)

    def chosen(slots, which):
        return jnp.sum(jnp.where(slot_of == which, slots.astype(F32), 0.0), axis=0)

    def row_copy(src, dst, send, recv, zz, xx):
        return pltpu.make_async_remote_copy(
            src_ref=src, dst_ref=dst, send_sem=send, recv_sem=recv,
            device_id=(zz * nx + xx, j), device_id_type=MESH,
        )

    def hop_copy(src, dst, k, h, row, col):
        return pltpu.make_async_remote_copy(
            src_ref=src, dst_ref=dst, send_sem=hop_send.at[k, h],
            recv_sem=hop_recv.at[k, h], device_id=(row, col), device_id_type=MESH,
        )

    def hop_wait(buf, k, h, slots):
        part = buf.at[pl.ds(0, slots)]
        hop_copy(part, part, k, h, i, j).wait()

    def cross_start(src, dst, k, h, target):
        def send(step, c):
            row, col = target(step)

            @pl.when((row != i) | (col != j))
            def _():
                hop_copy(src, dst, k, h, row, col).start()

            return c

        lax.fori_loop(0, n, send, 0)

    def cross_wait(buf, k, h):
        @pl.when(i == j)
        def _():
            hop_wait(buf, k, h, n - 1)

        @pl.when(i != j)
        def _():
            hop_wait(buf, k, h, n)

    def line_start(src, dst, k, h, target):
        def send(step, c):
            row, col = target(step)
            hop_copy(src(row, col), dst, k, h, row, col).start()
            return c

        lax.fori_loop(1, n, send, 0)

    def along_col(step):
        return i, (j + step) % n

    def along_row(step):
        return (i + step) % n, j

    def sums_col(k, h, value):
        out_s[k, h] = value
        in_s[k, h, j] = value
        line_start(lambda r, c: out_s.at[k, h], in_s.at[k, h, j], k, 4 + h, along_col)

    def sums_row(k, h):
        hop_wait(in_s.at[k, h], k, 4 + h, n - 1)
        value = jnp.sum(in_s[k, h], axis=0)
        out_s[k, h + 1] = value
        in_s[k, h + 1, i] = value
        line_start(lambda r, c: out_s.at[k, h + 1], in_s.at[k, h + 1, i], k, 5 + h, along_row)

    def sums_end(k, h):
        hop_wait(in_s.at[k, h + 1], k, 5 + h, n - 1)
        return jnp.sum(in_s[k, h + 1], axis=0)

    def spread_z(k, dz):
        return row_copy(
            gathered.at[k, z, x], gathered.at[k, z, x],
            gz_send.at[k, dz - 1], gz_recv.at[k, dz - 1], (z + dz) % nz, x,
        )

    def spread_x(k, dx, dz):
        zz = (z - dz + nz) % nz
        return row_copy(
            gathered.at[k, zz, x], gathered.at[k, zz, x],
            gx_send.at[k, dz, dx - 1], gx_recv.at[k, dz, dx - 1], z, (x + dx) % nx,
        )

    def forward_z(k, dz):
        spread_z(k, dz).wait()
        for dx in range(1, nx):
            spread_x(k, dx, dz).start()

    def start(k, residual):
        out1[k] = swap(jnp.sum(jnp.where(owned, residual, 0.0), axis=0)).astype(BF16)

        @pl.when(i == j)
        def _():
            in1[k, j] = out1[k]

        cross_start(out1.at[k], in1.at[k, j], k, 0, lambda step: ((i + step) % n, i))
        gathered[k, z, x] = residual.astype(BF16)
        for dz in range(1, nz):
            spread_z(k, dz).start()
        for dx in range(1, nx):
            spread_x(k, dx, 0).start()
        sums_col(k, 0, column_sums(residual * residual))

    sol_ref[...] = jnp.zeros_like(sol_ref)
    res_ref[...] = right_ref[...]
    direction[...] = jnp.zeros_like(direction)
    image[...] = jnp.zeros_like(image)
    slab_dir[...] = jnp.zeros_like(slab_dir)
    slab_img[...] = jnp.zeros_like(slab_img)
    start(0, right_ref[...])

    for a in range(block_rows):
        load(a).wait()
        slab_row = first + a * n + i

        def turn(q, c, a=a, slab_row=slab_row):
            at = pl.ds(pl.multiple_of(q * turn_rows, turn_rows), turn_rows)
            to = pl.ds(pl.multiple_of(a * order + q * turn_rows, turn_rows), turn_rows)
            for tile in range(blocks // 8):
                values = jnp.swapaxes(raw[a, at, tile * 8 : tile * 8 + 8, :], 0, 1)
                for b in range(8):
                    column = (tile * 8 + b) * n + j
                    weight = jnp.where(
                        column < slab_row, 1.0, jnp.where(column == slab_row, 0.5, 0.0)
                    )
                    matrix[tile * 8 + b, to] = values[b] * weight.astype(BF16)
            return c

        lax.fori_loop(0, order // turn_rows, turn, 0)

    def iteration(k, norm_old):
        residual = res_ref[...]
        cross_wait(in1.at[k], k, 0)
        out2[k] = chosen(in1[k], my_col).astype(BF16)
        in2[k, j] = out2[k]
        line_start(lambda r, c: out2.at[k], in2.at[k, j], k, 1, along_col)
        sums_row(k, 0)
        for dz in range(1, nz):
            forward_z(k, dz)
        hop_wait(in2.at[k], k, 1, n - 1)
        slab = in2[k].astype(F32).reshape(order, LANES)

        turned = jnp.transpose(slab).astype(BF16)
        both = jnp.concatenate([turned[0:HALF], turned[HALF:LANES]], axis=1)

        def mirror_x(chunk, dx):
            xx = (x + dx) % nx
            return row_copy(
                mirror.at[chunk, :, xx], got_x.at[k, chunk, dx - 1],
                mx_send.at[k, chunk, dx - 1], mx_recv.at[k, chunk, dx - 1], z, xx,
            )

        def mirror_z(chunk, dz):
            zz = (z + dz) % nz
            return row_copy(
                sums_z.at[chunk, zz], got_z.at[k, chunk, dz - 1],
                mz_send.at[k, chunk, dz - 1], mz_recv.at[k, chunk, dz - 1], zz, x,
            )

        def transposed(chunk, c):
            for u in range(per_chunk):
                p = chunk * per_chunk + u
                parts = [
                    jnp.dot(both, matrix[2 * p + h], preferred_element_type=F32)
                    for h in range(2)
                ]
                cells = jnp.transpose(jnp.concatenate(parts, axis=0))
                mirror[chunk, :, :, u] = cells.astype(BF16).reshape(nz, nx, CELLS, LANES)
            for dx in range(1, nx):
                mirror_x(chunk, dx).start()
            return c

        lax.fori_loop(0, CHUNKS, transposed, 0)

        norm = sums_end(k, 0)
        beta = jnp.where(k == 0, 0.0, norm / norm_old)
        slab_d = slab + beta * slab_dir[...]
        slab_dir[...] = slab_d
        beta_cell = beta.reshape(1, 1, LANES)
        cells_d = residual + beta_cell * direction[...]
        direction[...] = cells_d
        curve = column_sums(diag_ref[...] * cells_d * cells_d)

        for dz in range(nz):
            for dx in range(1, nx):
                spread_x(k, dx, dz).wait()
        rows = None
        for half in range(2):
            left, right = [], []
            for u in range(pairs // 2):
                p = half * (pairs // 2) + u
                cells = gathered[k, :, :, p].reshape(n, CELLS, LANES)
                left += [matrix[2 * p], matrix[2 * p + 1]]
                right += [
                    (cells * even_mask).reshape(order, LANES),
                    (cells * odd_mask).reshape(order, LANES),
                ]
            part = jnp.dot(
                jnp.concatenate(left, axis=1),
                jnp.concatenate(right, axis=0),
                preferred_element_type=F32,
            )
            rows = part if rows is None else rows + part
        rows = rows + pltpu.roll(rows, HALF, 1)
        rows = jnp.where(left_half, rows[0:order], rows[order:])

        out_a[k] = rows.astype(BF16).reshape(n, CELLS, LANES)
        in_a[k, j] = out_a[k, j]
        line_start(lambda r, c: out_a.at[k, c], in_a.at[k, j], k, 2, along_col)
        slab_q = rows + beta * slab_img[...]
        slab_img[...] = slab_q
        curve = curve + 2.0 * column_sums((slab_d * slab_q).reshape(n, CELLS, LANES))
        sums_col(k, 2, curve)

        def pass_z(chunk, c):
            for dx in range(1, nx):
                mirror_x(chunk, dx).wait()
            for dz in range(nz):
                zz = (z + dz) % nz
                total = mirror[chunk, zz, x].astype(F32)
                for dx in range(1, nx):
                    total = total + got_x[k, chunk, dx - 1, zz].astype(F32)
                sums_z[chunk, zz] = total.astype(BF16)
            for dz in range(1, nz):
                mirror_z(chunk, dz).start()
            return c

        lax.fori_loop(0, CHUNKS // 2, pass_z, 0)

        hop_wait(in_a.at[k], k, 2, n - 1)
        out_b[k] = jnp.sum(in_a[k].astype(F32), axis=0).astype(BF16)

        @pl.when(i == j)
        def _():
            in_b[k, i] = out_b[k]

        cross_start(out_b.at[k], in_b.at[k, i], k, 3, lambda step: (j, (j + step) % n))
        sums_row(k, 2)
        lax.fori_loop(CHUNKS // 2, CHUNKS, pass_z, 0)

        def finish_z(chunk, c):
            for dz in range(1, nz):
                mirror_z(chunk, dz).wait()
            at = pl.ds(chunk * per_chunk, per_chunk)
            total = sums_z[chunk, z].astype(F32)
            for dz in range(1, nz):
                total = total + got_z[k, chunk, dz - 1].astype(F32)
            image[at] = beta_cell * image[at] + total
            return c

        lax.fori_loop(0, CHUNKS, finish_z, 0)
        applied = image[...] + diag_ref[...] * residual

        cross_wait(in_b.at[k], k, 3)
        piece = swap(chosen(in_b[k], my_row))
        applied = applied + jnp.where(owned, piece.reshape(1, CELLS, LANES), 0.0)
        image[...] = applied
        length = (norm / sums_end(k, 2)).reshape(1, 1, LANES)
        sol_ref[...] = sol_ref[...] + length * cells_d
        residual = residual - length * applied
        res_ref[...] = residual

        @pl.when(k < ITERS - 1)
        def _():
            start(k + 1, residual)

        return norm

    lax.fori_loop(0, ITERS, iteration, jnp.ones((1, LANES), F32))


def body(nx, matrix, diagonal, right_side, slab_first):
    n = lax.axis_size("row")
    nz = n // nx
    rb, order, blocks, _ = matrix.shape
    cells, _, width = right_side.shape
    pairs = blocks // 2
    per_chunk = pairs // CHUNKS

    def packed(cell_array):
        return jnp.transpose(cell_array.reshape(cells, pairs, LANES), (1, 0, 2))

    def unpacked(cell_array):
        return jnp.transpose(cell_array, (1, 0, 2)).reshape(cells, blocks, width)

    diag = packed(jnp.broadcast_to(diagonal[:, :, None], right_side.shape))
    vec = (pairs, cells, LANES)
    part = (per_chunk, cells, LANES)
    piece = (cells, LANES)
    vmem = pl.BlockSpec(memory_space=pltpu.VMEM)
    dma = pltpu.SemaphoreType.DMA
    sol, res = pl.pallas_call(
        functools.partial(kernel, nx, nz),
        out_shape=[jax.ShapeDtypeStruct(vec, F32)] * 2,
        in_specs=[
            pl.BlockSpec(memory_space=pltpu.SMEM),
            pl.BlockSpec(memory_space=pl.ANY),
            vmem,
            vmem,
        ],
        out_specs=[vmem, vmem],
        scratch_shapes=[
            pltpu.VMEM(matrix.shape, BF16),
            pltpu.VMEM((blocks, rb * order, order), BF16),
            pltpu.VMEM((ITERS, nz, nx) + vec, BF16),
            pltpu.VMEM((CHUNKS, nz, nx) + part, BF16),
            pltpu.VMEM((ITERS, CHUNKS, nx - 1, nz) + part, BF16),
            pltpu.VMEM((CHUNKS, nz) + part, BF16),
            pltpu.VMEM((ITERS, CHUNKS, nz - 1) + part, BF16),
            pltpu.VMEM(vec, F32),
            pltpu.VMEM(vec, F32),
            pltpu.VMEM((order, LANES), F32),
            pltpu.VMEM((order, LANES), F32),
            pltpu.VMEM((ITERS,) + piece, BF16),
            pltpu.VMEM((ITERS, n) + piece, BF16),
            pltpu.VMEM((ITERS,) + piece, BF16),
            pltpu.VMEM((ITERS, n) + piece, BF16),
            pltpu.VMEM((ITERS, n) + piece, BF16),
            pltpu.VMEM((ITERS, n) + piece, BF16),
            pltpu.VMEM((ITERS,) + piece, BF16),
            pltpu.VMEM((ITERS, n) + piece, BF16),
            pltpu.VMEM((ITERS, 4, 1, LANES), F32),
            pltpu.VMEM((ITERS, 4, n, 1, LANES), F32),
            dma((rb,)),
            dma((ITERS, nz - 1)),
            dma((ITERS, nz - 1)),
            dma((ITERS, nz, nx - 1)),
            dma((ITERS, nz, nx - 1)),
            dma((ITERS, CHUNKS, nx - 1)),
            dma((ITERS, CHUNKS, nx - 1)),
            dma((ITERS, CHUNKS, nz - 1)),
            dma((ITERS, CHUNKS, nz - 1)),
            dma((ITERS, 8)),
            dma((ITERS, 8)),
        ],
        compiler_params=pltpu.CompilerParams(
            has_side_effects=True, vmem_limit_bytes=56 * 1024 * 1024
        ),
        name="conjugate_gradients",
    )(slab_first, matrix, diag, packed(right_side))
    return unpacked(sol), unpacked(res)


def solution(mesh, nx=NX):
    placed = (
        P(None, "row", None, "col"),
        P(("col", "row"), None),
        P(("col", "row"), None, None),
        P(),
    )
    return jax.shard_map(
        functools.partial(body, nx),
        mesh=mesh,
        in_specs=placed,
        out_specs=(P(("col", "row"), None, None), P(("col", "row"), None, None)),
        check_vma=False,
    )
```

```python
import functools

import jax
import jax.numpy as jnp
from jax import lax
from jax.experimental import pallas as pl
from jax.experimental.pallas import tpu as pltpu
from jax.sharding import PartitionSpec as P

ITERS = 3
NX = 4
CHUNKS = 4
ROWS = 32
MESH = pl.DeviceIdType.MESH
F32 = jnp.float32
BF16 = jnp.bfloat16
LANES = 128
HALF = 64
CELLS = 16


def column_sums(values):
    total = jnp.sum(jnp.sum(values, axis=0), axis=0, keepdims=True)
    return total + pltpu.roll(total, HALF, 1)


def kernel(
    nx, nz, live,
    first_ref, matrix_hbm, diag_ref, right_ref,
    sol_ref, res_ref,
    raw, matrix, gathered, mirror, got_x, sums_z, got_z,
    diagonal, direction, image, solution, residual_ref, slab_dir, slab_img,
    out1, in1, out2, in2, out_a, in_a, out_b, in_b, out_s, in_s,
    load_sem, gz_send, gz_recv, gx_send, gx_recv,
    mx_send, mx_recv, mz_send, mz_recv, hop_send, hop_recv,
):
    n = nx * nz
    pairs = diagonal.shape[0]
    order = n * CELLS
    block_rows = raw.shape[0]
    stored = raw.shape[2]
    per_chunk = live // CHUNKS
    turn_rows = min(ROWS, order)
    i = lax.axis_index("row")
    j = lax.axis_index("col")
    z = i // nx
    x = i % nx
    first = first_ref[0]
    my_row = (j - first) & (n - 1)
    my_block = (first + my_row) // n
    my_col = (first + i) & (n - 1)
    odd = (my_block & 1) == 1

    def load(a):
        return pltpu.make_async_copy(
            matrix_hbm.at[a, :, pl.ds(0, stored)], raw.at[a], load_sem.at[a]
        )

    for a in range(block_rows):
        load(a).start()

    block_of = (
        2 * lax.broadcasted_iota(jnp.int32, (pairs, CELLS, LANES), 0)
        + lax.broadcasted_iota(jnp.int32, (pairs, CELLS, LANES), 2) // HALF
    )
    owned = (block_of == my_block) | (block_of == my_block + 1)
    slot_of = lax.broadcasted_iota(jnp.int32, (n, CELLS, LANES), 0)
    left_half = lax.broadcasted_iota(jnp.int32, (order, LANES), 1) < HALF
    even_lanes = (lax.broadcasted_iota(jnp.int32, (CELLS, LANES), 1) < HALF).astype(F32)
    even_mask = even_lanes.astype(BF16)
    odd_mask = (1.0 - even_lanes).astype(BF16)

    def swap(piece):
        return jnp.where(odd, pltpu.roll(piece, HALF, 1), piece)

    def chosen(slots, which):
        return jnp.sum(jnp.where(slot_of == which, slots.astype(F32), 0.0), axis=0)

    def row_copy(src, dst, send, recv, zz, xx):
        return pltpu.make_async_remote_copy(
            src_ref=src, dst_ref=dst, send_sem=send, recv_sem=recv,
            device_id=(zz * nx + xx, j), device_id_type=MESH,
        )

    def hop_copy(src, dst, k, h, row, col):
        return pltpu.make_async_remote_copy(
            src_ref=src, dst_ref=dst, send_sem=hop_send.at[k, h],
            recv_sem=hop_recv.at[k, h], device_id=(row, col), device_id_type=MESH,
        )

    def hop_wait(buf, k, h, slots):
        part = buf.at[pl.ds(0, slots)]
        hop_copy(part, part, k, h, i, j).wait()

    def cross_start(src, dst, k, h, target):
        def send(step, c):
            row, col = target(step)

            @pl.when((row != i) | (col != j))
            def _():
                hop_copy(src, dst, k, h, row, col).start()

            return c

        lax.fori_loop(0, n, send, 0)

    def cross_wait(buf, k, h):
        @pl.when(i == j)
        def _():
            hop_wait(buf, k, h, n - 1)

        @pl.when(i != j)
        def _():
            hop_wait(buf, k, h, n)

    def line_start(src, dst, k, h, target):
        def send(step, c):
            row, col = target(step)
            hop_copy(src(row, col), dst, k, h, row, col).start()
            return c

        lax.fori_loop(1, n, send, 0)

    def along_col(step):
        return i, (j + step) % n

    def along_row(step):
        return (i + step) % n, j

    def sums_col(k, h, value):
        out_s[k, h] = value
        in_s[k, h, j] = value
        line_start(lambda r, c: out_s.at[k, h], in_s.at[k, h, j], k, 4 + h, along_col)

    def sums_row(k, h):
        hop_wait(in_s.at[k, h], k, 4 + h, n - 1)
        value = jnp.sum(in_s[k, h], axis=0)
        out_s[k, h + 1] = value
        in_s[k, h + 1, i] = value
        line_start(lambda r, c: out_s.at[k, h + 1], in_s.at[k, h + 1, i], k, 5 + h, along_row)

    def sums_end(k, h):
        hop_wait(in_s.at[k, h + 1], k, 5 + h, n - 1)
        return jnp.sum(in_s[k, h + 1], axis=0)

    def spread_z(k, dz):
        return row_copy(
            gathered.at[k, z, x], gathered.at[k, z, x],
            gz_send.at[k, dz - 1], gz_recv.at[k, dz - 1], (z + dz) % nz, x,
        )

    def spread_x(k, dx, dz):
        zz = (z - dz + nz) % nz
        return row_copy(
            gathered.at[k, zz, x], gathered.at[k, zz, x],
            gx_send.at[k, dz, dx - 1], gx_recv.at[k, dz, dx - 1], z, (x + dx) % nx,
        )

    def forward_z(k, dz):
        spread_z(k, dz).wait()
        for dx in range(1, nx):
            spread_x(k, dx, dz).start()

    def start(k, residual):
        out1[k] = swap(jnp.sum(jnp.where(owned, residual, 0.0), axis=0)).astype(BF16)

        @pl.when(i == j)
        def _():
            in1[k, j] = out1[k]

        cross_start(out1.at[k], in1.at[k, j], k, 0, lambda step: ((j + step) % n, i))
        gathered[k, z, x] = residual[0:live].astype(BF16)
        for dz in range(1, nz):
            spread_z(k, dz).start()
        for dx in range(1, nx):
            spread_x(k, dx, 0).start()
        sums_col(k, 0, column_sums(residual * residual))

    for tile in range(2 * pairs // 8):
        values = jnp.swapaxes(right_ref[:, tile * 8 : tile * 8 + 8, :], 0, 1)
        for u in range(4):
            at = tile * 4 + u
            residual_ref[at] = jnp.concatenate([values[2 * u], values[2 * u + 1]], axis=1)
            diagonal[at] = jnp.concatenate(
                [
                    jnp.broadcast_to(diag_ref[:, 2 * at + h : 2 * at + h + 1], (CELLS, HALF))
                    for h in range(2)
                ],
                axis=1,
            )
    solution[...] = jnp.zeros_like(solution)
    direction[...] = jnp.zeros_like(direction)
    image[...] = jnp.zeros_like(image)
    slab_dir[...] = jnp.zeros_like(slab_dir)
    slab_img[...] = jnp.zeros_like(slab_img)
    start(0, residual_ref[...])

    for a in range(block_rows):
        load(a).wait()
        slab_row = first + a * n + i

        def turn(q, c, a=a, slab_row=slab_row):
            at = pl.ds(pl.multiple_of(q * turn_rows, turn_rows), turn_rows)
            to = pl.ds(pl.multiple_of(a * order + q * turn_rows, turn_rows), turn_rows)
            for tile in range(live // 4):
                values = jnp.swapaxes(raw[a, at, tile * 8 : tile * 8 + 8, :], 0, 1)
                for b in range(8):
                    column = (tile * 8 + b) * n + j
                    weight = jnp.where(
                        column < slab_row, 1.0, jnp.where(column == slab_row, 0.5, 0.0)
                    )
                    matrix[tile * 8 + b, to] = values[b] * weight.astype(BF16)
            return c

        lax.fori_loop(0, order // turn_rows, turn, 0)

    def iteration(k, norm_old):
        residual = residual_ref[...]
        forward_z(k, 1)
        if nz > 2:
            forward_z(k, nz - 1)
        cross_wait(in1.at[k], k, 0)
        out2[k] = chosen(in1[k], my_col).astype(BF16)
        in2[k, j] = out2[k]
        line_start(lambda r, c: out2.at[k], in2.at[k, j], k, 1, along_col)
        for dz in range(2, nz - 1):
            forward_z(k, dz)
        sums_row(k, 0)
        hop_wait(in2.at[k], k, 1, n - 1)
        slab = in2[k].astype(F32).reshape(order, LANES)

        turned = jnp.transpose(slab).astype(BF16)
        both = jnp.concatenate([turned[0:HALF], turned[HALF:LANES]], axis=1)

        def mirror_x(chunk, dx):
            xx = (x + dx) % nx
            return row_copy(
                mirror.at[chunk, :, xx], got_x.at[k, chunk, dx - 1],
                mx_send.at[k, chunk, dx - 1], mx_recv.at[k, chunk, dx - 1], z, xx,
            )

        def mirror_z(chunk, dz):
            zz = (z + dz) % nz
            return row_copy(
                sums_z.at[chunk, zz], got_z.at[k, chunk, dz - 1],
                mz_send.at[k, chunk, dz - 1], mz_recv.at[k, chunk, dz - 1], zz, x,
            )

        def transposed(chunk, c):
            for u in range(per_chunk):
                p = chunk * per_chunk + u
                parts = [
                    jnp.dot(both, matrix[2 * p + h], preferred_element_type=F32)
                    for h in range(2)
                ]
                cells = jnp.transpose(jnp.concatenate(parts, axis=0))
                mirror[chunk, :, :, u] = cells.astype(BF16).reshape(nz, nx, CELLS, LANES)
            for dx in range(1, nx):
                mirror_x(chunk, dx).start()
            return c

        lax.fori_loop(0, CHUNKS, transposed, 0)

        norm = sums_end(k, 0)
        beta = jnp.where(k == 0, 0.0, norm / norm_old)
        slab_d = slab + beta * slab_dir[...]
        slab_dir[...] = slab_d
        beta_cell = beta.reshape(1, 1, LANES)
        cells_d = residual + beta_cell * direction[...]
        direction[...] = cells_d
        curve = column_sums(diagonal[...] * cells_d * cells_d)

        for dz in range(nz):
            for dx in range(1, nx):
                spread_x(k, dx, dz).wait()
        rows = None
        for half in range(2):
            left, right = [], []
            for u in range(live // 2):
                p = half * (live // 2) + u
                cells = gathered[k, :, :, p].reshape(n, CELLS, LANES)
                left += [matrix[2 * p], matrix[2 * p + 1]]
                right += [
                    (cells * even_mask).reshape(order, LANES),
                    (cells * odd_mask).reshape(order, LANES),
                ]
            part = jnp.dot(
                jnp.concatenate(left, axis=1),
                jnp.concatenate(right, axis=0),
                preferred_element_type=F32,
            )
            rows = part if rows is None else rows + part
        rows = rows + pltpu.roll(rows, HALF, 1)
        rows = jnp.where(left_half, rows[0:order], rows[order:])

        out_a[k] = rows.astype(BF16).reshape(n, CELLS, LANES)
        in_a[k, j] = out_a[k, j]
        line_start(lambda r, c: out_a.at[k, c], in_a.at[k, j], k, 2, along_col)
        slab_q = rows + beta * slab_img[...]
        slab_img[...] = slab_q
        curve = curve + 2.0 * column_sums((slab_d * slab_q).reshape(n, CELLS, LANES))
        sums_col(k, 2, curve)

        def pass_z(chunk, c):
            for dx in range(1, nx):
                mirror_x(chunk, dx).wait()
            for dz in range(nz):
                zz = (z + dz) % nz
                total = mirror[chunk, zz, x].astype(F32)
                for dx in range(1, nx):
                    total = total + got_x[k, chunk, dx - 1, zz].astype(F32)
                sums_z[chunk, zz] = total.astype(BF16)
            for dz in range(1, nz):
                mirror_z(chunk, dz).start()
            return c

        lax.fori_loop(0, CHUNKS // 2, pass_z, 0)

        hop_wait(in_a.at[k], k, 2, n - 1)
        out_b[k] = jnp.sum(in_a[k].astype(F32), axis=0).astype(BF16)

        @pl.when(i == j)
        def _():
            in_b[k, i] = out_b[k]

        cross_start(out_b.at[k], in_b.at[k, i], k, 3, lambda step: (j, (i + step) % n))
        sums_row(k, 2)
        lax.fori_loop(CHUNKS // 2, CHUNKS, pass_z, 0)

        def finish_z(chunk, c):
            for dz in range(1, nz):
                mirror_z(chunk, dz).wait()
            at = pl.ds(chunk * per_chunk, per_chunk)
            total = sums_z[chunk, z].astype(F32)
            for dz in range(1, nz):
                total = total + got_z[k, chunk, dz - 1].astype(F32)
            image[at] = image[at] + total
            return c

        image[...] = beta_cell * image[...] + diagonal[...] * residual
        lax.fori_loop(0, CHUNKS, finish_z, 0)
        applied = image[...]

        cross_wait(in_b.at[k], k, 3)
        piece = swap(chosen(in_b[k], my_row))
        applied = applied + jnp.where(owned, piece.reshape(1, CELLS, LANES), 0.0)
        image[...] = applied
        length = (norm / sums_end(k, 2)).reshape(1, 1, LANES)
        solution[...] = solution[...] + length * cells_d
        residual = residual - length * applied
        residual_ref[...] = residual

        @pl.when(k < ITERS - 1)
        def _():
            start(k + 1, residual)

        return norm

    lax.fori_loop(0, ITERS, iteration, jnp.ones((1, LANES), F32))
    for source, target in ((solution, sol_ref), (residual_ref, res_ref)):
        for tile in range(2 * pairs // 8):
            halves = []
            for u in range(4):
                values = source[tile * 4 + u]
                halves += [values[:, 0:HALF], values[:, HALF:LANES]]
            target[:, tile * 8 : tile * 8 + 8, :] = jnp.swapaxes(jnp.stack(halves), 0, 1)


def body(nx, matrix, diagonal, right_side, slab_first):
    n = lax.axis_size("row")
    nz = n // nx
    rb, order, blocks, _ = matrix.shape
    cells = right_side.shape[0]
    pairs = blocks // 2
    vec = (pairs, cells, LANES)
    piece = (cells, LANES)
    vmem = pl.BlockSpec(memory_space=pltpu.VMEM)
    dma = pltpu.SemaphoreType.DMA

    def solve(live):
        stored = min(blocks, -(-2 * live // 16) * 16)
        shard = (live, cells, LANES)
        part = (live // CHUNKS, cells, LANES)
        return pl.pallas_call(
            functools.partial(kernel, nx, nz, live),
            out_shape=[jax.ShapeDtypeStruct(right_side.shape, F32)] * 2,
            in_specs=[
                pl.BlockSpec(memory_space=pltpu.SMEM),
                pl.BlockSpec(memory_space=pl.ANY),
                vmem,
                vmem,
            ],
            out_specs=[vmem, vmem],
            scratch_shapes=[
                pltpu.VMEM((rb, order, stored, order), BF16),
                pltpu.VMEM((2 * live, rb * order, order), BF16),
                pltpu.VMEM((ITERS, nz, nx) + shard, BF16),
                pltpu.VMEM((CHUNKS, nz, nx) + part, BF16),
                pltpu.VMEM((ITERS, CHUNKS, nx - 1, nz) + part, BF16),
                pltpu.VMEM((CHUNKS, nz) + part, BF16),
                pltpu.VMEM((ITERS, CHUNKS, nz - 1) + part, BF16),
                pltpu.VMEM(vec, F32),
                pltpu.VMEM(vec, F32),
                pltpu.VMEM(vec, F32),
                pltpu.VMEM(vec, F32),
                pltpu.VMEM(vec, F32),
                pltpu.VMEM((order, LANES), F32),
                pltpu.VMEM((order, LANES), F32),
                pltpu.VMEM((ITERS,) + piece, BF16),
                pltpu.VMEM((ITERS, n) + piece, BF16),
                pltpu.VMEM((ITERS,) + piece, BF16),
                pltpu.VMEM((ITERS, n) + piece, BF16),
                pltpu.VMEM((ITERS, n) + piece, BF16),
                pltpu.VMEM((ITERS, n) + piece, BF16),
                pltpu.VMEM((ITERS,) + piece, BF16),
                pltpu.VMEM((ITERS, n) + piece, BF16),
                pltpu.VMEM((ITERS, 4, 1, LANES), F32),
                pltpu.VMEM((ITERS, 4, n, 1, LANES), F32),
                dma((rb,)),
                dma((ITERS, nz - 1)),
                dma((ITERS, nz - 1)),
                dma((ITERS, nz, nx - 1)),
                dma((ITERS, nz, nx - 1)),
                dma((ITERS, CHUNKS, nx - 1)),
                dma((ITERS, CHUNKS, nx - 1)),
                dma((ITERS, CHUNKS, nz - 1)),
                dma((ITERS, CHUNKS, nz - 1)),
                dma((ITERS, 8)),
                dma((ITERS, 8)),
            ],
            compiler_params=pltpu.CompilerParams(
                has_side_effects=True, vmem_limit_bytes=56 * 1024 * 1024
            ),
            name=f"conjugate_gradients_{live}",
        )(slab_first, matrix, diagonal, right_side)

    lives = range(CHUNKS, pairs + 1, CHUNKS)
    used = (slab_first[0] + rb * n - 1) // n + 1
    branch = jnp.clip((used + 2 * CHUNKS - 1) // (2 * CHUNKS) - 1, 0, len(lives) - 1)
    return lax.switch(branch, [functools.partial(solve, live) for live in lives])


def solution(mesh, nx=NX):
    placed = (
        P(None, "row", None, "col"),
        P(("col", "row"), None),
        P(("col", "row"), None, None),
        P(),
    )
    return jax.shard_map(
        functools.partial(body, nx),
        mesh=mesh,
        in_specs=placed,
        out_specs=(P(("col", "row"), None, None), P(("col", "row"), None, None)),
        check_vma=False,
    )
```

```python
import functools

import jax
import jax.numpy as jnp
from jax import lax
from jax.experimental import pallas as pl
from jax.experimental.pallas import tpu as pltpu
from jax.sharding import PartitionSpec as P

ITERS = 3
NX = 4
CHUNKS = 4
ROWS = 32
MESH = pl.DeviceIdType.MESH
F32 = jnp.float32
BF16 = jnp.bfloat16
LANES = 128
HALF = 64
CELLS = 16


def column_sums(values):
    total = jnp.sum(jnp.sum(values, axis=0), axis=0, keepdims=True)
    return total + pltpu.roll(total, HALF, 1)


def kernel(
    nx, nz, live,
    first_ref, matrix_hbm, diag_ref, right_ref,
    sol_ref, res_ref,
    raw, matrix, gathered, mirror, got_x, sums_z, got_z, first_z, sums_x, last_x,
    diagonal, direction, image, solution, residual_ref, slab_dir, slab_img,
    out1, in1, out2, in2, out_a, in_a, out_b, in_b, out_s, in_s,
    load_sem, gz_send, gz_recv, gx_send, gx_recv,
    mx_send, mx_recv, mz_send, mz_recv, fz_send, fz_recv, lx_send, lx_recv, hop_send, hop_recv,
):
    n = nx * nz
    pairs = diagonal.shape[0]
    order = n * CELLS
    block_rows = raw.shape[0]
    stored = raw.shape[2]
    per_chunk = live // CHUNKS
    turn_rows = min(ROWS, order)
    i = lax.axis_index("row")
    j = lax.axis_index("col")
    z = i // nx
    x = i % nx
    first = first_ref[0]
    my_row = (j - first) & (n - 1)
    my_block = (first + my_row) // n
    shift = first & (n - 1)
    odd = (my_block & 1) == 1

    def load(a):
        return pltpu.make_async_copy(
            matrix_hbm.at[a, :, pl.ds(0, stored)], raw.at[a], load_sem.at[a]
        )

    for a in range(block_rows):
        load(a).start()

    block_of = (
        2 * lax.broadcasted_iota(jnp.int32, (pairs, CELLS, LANES), 0)
        + lax.broadcasted_iota(jnp.int32, (pairs, CELLS, LANES), 2) // HALF
    )
    owned = (block_of == my_block) | (block_of == my_block + 1)
    left_half = lax.broadcasted_iota(jnp.int32, (order, LANES), 1) < HALF
    even_lanes = (lax.broadcasted_iota(jnp.int32, (CELLS, LANES), 1) < HALF).astype(F32)
    even_mask = even_lanes.astype(BF16)
    odd_mask = (1.0 - even_lanes).astype(BF16)

    def swap(piece):
        return jnp.where(odd, pltpu.roll(piece, HALF, 1), piece)

    def rotated(slots, back):
        slots = slots.astype(F32)
        step = 1
        while step < n:
            cut = n - step if back else step
            moved = jnp.concatenate([slots[cut:], slots[:cut]], axis=0)
            slots = jnp.where((shift & step) != 0, moved, slots)
            step *= 2
        return slots.astype(BF16)

    def row_copy(src, dst, send, recv, zz, xx):
        return pltpu.make_async_remote_copy(
            src_ref=src, dst_ref=dst, send_sem=send, recv_sem=recv,
            device_id=(zz * nx + xx, j), device_id_type=MESH,
        )

    def hop_copy(src, dst, k, h, row, col):
        return pltpu.make_async_remote_copy(
            src_ref=src, dst_ref=dst, send_sem=hop_send.at[k, h],
            recv_sem=hop_recv.at[k, h], device_id=(row, col), device_id_type=MESH,
        )

    def hop_wait(buf, k, h, slots):
        part = buf.at[pl.ds(0, slots)]
        hop_copy(part, part, k, h, i, j).wait()

    def line_start(src, dst, k, h, target):
        def send(step, c):
            row, col = target(step)
            hop_copy(src(row, col), dst, k, h, row, col).start()
            return c

        lax.fori_loop(1, n, send, 0)

    def along_col(step):
        return i, (j + step) % n

    def along_row(step):
        return (i + step) % n, j

    def sums_col(k, h, value):
        out_s[k, h] = value
        in_s[k, h, j] = value
        line_start(lambda r, c: out_s.at[k, h], in_s.at[k, h, j], k, 4 + h, along_col)

    def sums_row(k, h):
        hop_wait(in_s.at[k, h], k, 4 + h, n - 1)
        value = jnp.sum(in_s[k, h], axis=0)
        out_s[k, h + 1] = value
        in_s[k, h + 1, i] = value
        line_start(lambda r, c: out_s.at[k, h + 1], in_s.at[k, h + 1, i], k, 5 + h, along_row)

    def sums_end(k, h):
        hop_wait(in_s.at[k, h + 1], k, 5 + h, n - 1)
        return jnp.sum(in_s[k, h + 1], axis=0)

    def spread_z(k, dz):
        return row_copy(
            gathered.at[k, z, x], gathered.at[k, z, x],
            gz_send.at[k, dz - 1], gz_recv.at[k, dz - 1], (z + dz) % nz, x,
        )

    def spread_x(k, dx, dz):
        zz = (z - dz + nz) % nz
        return row_copy(
            gathered.at[k, zz, x], gathered.at[k, zz, x],
            gx_send.at[k, dz, dx - 1], gx_recv.at[k, dz, dx - 1], z, (x + dx) % nx,
        )

    def forward_z(k, dz):
        spread_z(k, dz).wait()
        for dx in range(1, nx):
            spread_x(k, dx, dz).start()

    def start(k, residual):
        out1[k] = swap(jnp.sum(jnp.where(owned, residual, 0.0), axis=0)).astype(BF16)
        in1[k, j] = out1[k]
        line_start(lambda r, c: out1.at[k], in1.at[k, j], k, 0, along_col)
        gathered[k, z, x] = residual[0:live].astype(BF16)
        for dz in range(1, nz):
            spread_z(k, dz).start()
        for dx in range(1, nx):
            spread_x(k, dx, 0).start()
        sums_col(k, 0, column_sums(residual * residual))

    for tile in range(2 * pairs // 8):
        values = jnp.swapaxes(right_ref[:, tile * 8 : tile * 8 + 8, :], 0, 1)
        for u in range(4):
            at = tile * 4 + u
            residual_ref[at] = jnp.concatenate([values[2 * u], values[2 * u + 1]], axis=1)
            diagonal[at] = jnp.concatenate(
                [
                    jnp.broadcast_to(diag_ref[:, 2 * at + h : 2 * at + h + 1], (CELLS, HALF))
                    for h in range(2)
                ],
                axis=1,
            )
    solution[...] = jnp.zeros_like(solution)
    direction[...] = jnp.zeros_like(direction)
    image[...] = jnp.zeros_like(image)
    slab_dir[...] = jnp.zeros_like(slab_dir)
    slab_img[...] = jnp.zeros_like(slab_img)
    start(0, residual_ref[...])

    for a in range(block_rows):
        load(a).wait()
        slab_row = first + a * n + i

        def turn(q, c, a=a, slab_row=slab_row):
            at = pl.ds(pl.multiple_of(q * turn_rows, turn_rows), turn_rows)
            to = pl.ds(pl.multiple_of(a * order + q * turn_rows, turn_rows), turn_rows)
            for tile in range(live // 4):
                values = jnp.swapaxes(raw[a, at, tile * 8 : tile * 8 + 8, :], 0, 1)
                for b in range(8):
                    column = (tile * 8 + b) * n + j
                    weight = jnp.where(
                        column < slab_row, 1.0, jnp.where(column == slab_row, 0.5, 0.0)
                    )
                    matrix[tile * 8 + b, to] = values[b] * weight.astype(BF16)
            return c

        lax.fori_loop(0, order // turn_rows, turn, 0)

    def iteration(k, norm_old):
        residual = residual_ref[...]
        forward_z(k, 1)
        if nz > 2:
            forward_z(k, nz - 1)
        hop_wait(in1.at[k], k, 0, n - 1)
        out2[k] = rotated(in1[k], False)
        in2[k, i] = out2[k, i]
        line_start(lambda r, c: out2.at[k, r], in2.at[k, i], k, 1, along_row)
        for dz in range(2, nz - 1):
            forward_z(k, dz)
        sums_row(k, 0)
        hop_wait(in2.at[k], k, 1, n - 1)
        slab = in2[k].astype(F32).reshape(order, LANES)

        turned = jnp.transpose(slab).astype(BF16)
        both = jnp.concatenate([turned[0:HALF], turned[HALF:LANES]], axis=1)

        def mirror_x(chunk, dx):
            xx = (x + dx) % nx
            return row_copy(
                mirror.at[chunk, :, xx], got_x.at[k, chunk, dx - 1],
                mx_send.at[k, chunk, dx - 1], mx_recv.at[k, chunk, dx - 1], z, xx,
            )

        def mirror_z(chunk, dz):
            zz = (z + dz) % nz
            return row_copy(
                sums_z.at[chunk, zz], got_z.at[k, chunk, dz - 1],
                mz_send.at[k, chunk, dz - 1], mz_recv.at[k, chunk, dz - 1], zz, x,
            )

        def early_z(dz):
            zz = (z + dz) % nz
            return row_copy(
                mirror.at[0, zz], first_z.at[k, dz - 1],
                fz_send.at[k, dz - 1], fz_recv.at[k, dz - 1], zz, x,
            )

        def late_x(dx):
            xx = (x + dx) % nx
            return row_copy(
                sums_x.at[xx], last_x.at[k, dx - 1],
                lx_send.at[k, dx - 1], lx_recv.at[k, dx - 1], z, xx,
            )

        def pass_x():
            for dz in range(1, nz):
                early_z(dz).wait()
            for xx in range(nx):
                total = mirror[0, z, xx].astype(F32)
                for dz in range(1, nz):
                    total = total + first_z[k, dz - 1, xx].astype(F32)
                sums_x[xx] = total.astype(BF16)
            for dx in range(1, nx):
                late_x(dx).start()

        def transposed(chunk):
            for u in range(per_chunk):
                p = chunk * per_chunk + u
                parts = [
                    jnp.dot(both, matrix[2 * p + h], preferred_element_type=F32)
                    for h in range(2)
                ]
                cells = jnp.transpose(jnp.concatenate(parts, axis=0))
                mirror[chunk, :, :, u] = cells.astype(BF16).reshape(nz, nx, CELLS, LANES)

        def transposed_x(chunk, c):
            transposed(chunk)
            for dx in range(1, nx):
                mirror_x(chunk, dx).start()
            return c

        transposed(0)
        for dz in range(1, nz):
            early_z(dz).start()
        lax.fori_loop(1, CHUNKS, transposed_x, 0)

        def pass_z(chunk, c):
            for dx in range(1, nx):
                mirror_x(chunk, dx).wait()
            for dz in range(nz):
                zz = (z + dz) % nz
                total = mirror[chunk, zz, x].astype(F32)
                for dx in range(1, nx):
                    total = total + got_x[k, chunk, dx - 1, zz].astype(F32)
                sums_z[chunk, zz] = total.astype(BF16)
            for dz in range(1, nz):
                mirror_z(chunk, dz).start()
            return c

        norm = sums_end(k, 0)
        beta = jnp.where(k == 0, 0.0, norm / norm_old)
        slab_d = slab + beta * slab_dir[...]
        slab_dir[...] = slab_d
        beta_cell = beta.reshape(1, 1, LANES)
        cells_d = residual + beta_cell * direction[...]
        direction[...] = cells_d
        curve = column_sums(diagonal[...] * cells_d * cells_d)

        for dz in range(nz):
            for dx in range(1, nx):
                spread_x(k, dx, dz).wait()
        rows = None
        for half in range(2):
            left, right = [], []
            for u in range(live // 2):
                p = half * (live // 2) + u
                cells = gathered[k, :, :, p].reshape(n, CELLS, LANES)
                left += [matrix[2 * p], matrix[2 * p + 1]]
                right += [
                    (cells * even_mask).reshape(order, LANES),
                    (cells * odd_mask).reshape(order, LANES),
                ]
            part = jnp.dot(
                jnp.concatenate(left, axis=1),
                jnp.concatenate(right, axis=0),
                preferred_element_type=F32,
            )
            rows = part if rows is None else rows + part
        rows = rows + pltpu.roll(rows, HALF, 1)
        rows = jnp.where(left_half, rows[0:order], rows[order:])

        out_a[k] = rows.astype(BF16).reshape(n, CELLS, LANES)
        in_a[k, i] = out_a[k, i]
        line_start(lambda r, c: out_a.at[k, r], in_a.at[k, i], k, 2, along_row)
        slab_q = rows + beta * slab_img[...]
        slab_img[...] = slab_q
        curve = curve + 2.0 * column_sums((slab_d * slab_q).reshape(n, CELLS, LANES))
        sums_col(k, 2, curve)

        pass_x()
        pass_z(1, 0)
        pass_z(2, 0)

        hop_wait(in_a.at[k], k, 2, n - 1)
        out_b[k] = rotated(in_a[k], True)
        in_b[k, j] = out_b[k, j]
        line_start(lambda r, c: out_b.at[k, c], in_b.at[k, j], k, 3, along_col)
        sums_row(k, 2)
        pass_z(3, 0)

        def finish_z(chunk, c):
            for dz in range(1, nz):
                mirror_z(chunk, dz).wait()
            at = pl.ds(chunk * per_chunk, per_chunk)
            total = sums_z[chunk, z].astype(F32)
            for dz in range(1, nz):
                total = total + got_z[k, chunk, dz - 1].astype(F32)
            image[at] = image[at] + total
            return c

        image[...] = beta_cell * image[...] + diagonal[...] * residual
        lax.fori_loop(1, CHUNKS, finish_z, 0)
        for dx in range(1, nx):
            late_x(dx).wait()
        total = sums_x[x].astype(F32)
        for dx in range(1, nx):
            total = total + last_x[k, dx - 1].astype(F32)
        image[0:per_chunk] = image[0:per_chunk] + total
        applied = image[...]

        hop_wait(in_b.at[k], k, 3, n - 1)
        piece = swap(jnp.sum(in_b[k].astype(F32), axis=0))
        applied = applied + jnp.where(owned, piece.reshape(1, CELLS, LANES), 0.0)
        image[...] = applied
        length = (norm / sums_end(k, 2)).reshape(1, 1, LANES)
        solution[...] = solution[...] + length * cells_d
        residual = residual - length * applied
        residual_ref[...] = residual

        @pl.when(k < ITERS - 1)
        def _():
            start(k + 1, residual)

        return norm

    lax.fori_loop(0, ITERS, iteration, jnp.ones((1, LANES), F32))
    for source, target in ((solution, sol_ref), (residual_ref, res_ref)):
        for tile in range(2 * pairs // 8):
            halves = []
            for u in range(4):
                values = source[tile * 4 + u]
                halves += [values[:, 0:HALF], values[:, HALF:LANES]]
            target[:, tile * 8 : tile * 8 + 8, :] = jnp.swapaxes(jnp.stack(halves), 0, 1)


def body(nx, matrix, diagonal, right_side, slab_first):
    n = lax.axis_size("row")
    nz = n // nx
    rb, order, blocks, _ = matrix.shape
    cells = right_side.shape[0]
    pairs = blocks // 2
    vec = (pairs, cells, LANES)
    piece = (cells, LANES)
    vmem = pl.BlockSpec(memory_space=pltpu.VMEM)
    dma = pltpu.SemaphoreType.DMA

    def solve(live):
        stored = min(blocks, -(-2 * live // 16) * 16)
        shard = (live, cells, LANES)
        part = (live // CHUNKS, cells, LANES)
        return pl.pallas_call(
            functools.partial(kernel, nx, nz, live),
            out_shape=[jax.ShapeDtypeStruct(right_side.shape, F32)] * 2,
            in_specs=[
                pl.BlockSpec(memory_space=pltpu.SMEM),
                pl.BlockSpec(memory_space=pl.ANY),
                vmem,
                vmem,
            ],
            out_specs=[vmem, vmem],
            scratch_shapes=[
                pltpu.VMEM((rb, order, stored, order), BF16),
                pltpu.VMEM((2 * live, rb * order, order), BF16),
                pltpu.VMEM((ITERS, nz, nx) + shard, BF16),
                pltpu.VMEM((CHUNKS, nz, nx) + part, BF16),
                pltpu.VMEM((ITERS, CHUNKS, nx - 1, nz) + part, BF16),
                pltpu.VMEM((CHUNKS, nz) + part, BF16),
                pltpu.VMEM((ITERS, CHUNKS, nz - 1) + part, BF16),
                pltpu.VMEM((ITERS, nz - 1, nx) + part, BF16),
                pltpu.VMEM((nx,) + part, BF16),
                pltpu.VMEM((ITERS, nx - 1) + part, BF16),
                pltpu.VMEM(vec, F32),
                pltpu.VMEM(vec, F32),
                pltpu.VMEM(vec, F32),
                pltpu.VMEM(vec, F32),
                pltpu.VMEM(vec, F32),
                pltpu.VMEM((order, LANES), F32),
                pltpu.VMEM((order, LANES), F32),
                pltpu.VMEM((ITERS,) + piece, BF16),
                pltpu.VMEM((ITERS, n) + piece, BF16),
                pltpu.VMEM((ITERS, n) + piece, BF16),
                pltpu.VMEM((ITERS, n) + piece, BF16),
                pltpu.VMEM((ITERS, n) + piece, BF16),
                pltpu.VMEM((ITERS, n) + piece, BF16),
                pltpu.VMEM((ITERS, n) + piece, BF16),
                pltpu.VMEM((ITERS, n) + piece, BF16),
                pltpu.VMEM((ITERS, 4, 1, LANES), F32),
                pltpu.VMEM((ITERS, 4, n, 1, LANES), F32),
                dma((rb,)),
                dma((ITERS, nz - 1)),
                dma((ITERS, nz - 1)),
                dma((ITERS, nz, nx - 1)),
                dma((ITERS, nz, nx - 1)),
                dma((ITERS, CHUNKS, nx - 1)),
                dma((ITERS, CHUNKS, nx - 1)),
                dma((ITERS, CHUNKS, nz - 1)),
                dma((ITERS, CHUNKS, nz - 1)),
                dma((ITERS, nz - 1)),
                dma((ITERS, nz - 1)),
                dma((ITERS, nx - 1)),
                dma((ITERS, nx - 1)),
                dma((ITERS, 8)),
                dma((ITERS, 8)),
            ],
            compiler_params=pltpu.CompilerParams(
                has_side_effects=True, vmem_limit_bytes=56 * 1024 * 1024
            ),
            name=f"conjugate_gradients_{live}",
        )(slab_first, matrix, diagonal, right_side)

    lives = range(CHUNKS, pairs + 1, CHUNKS)
    used = (slab_first[0] + rb * n - 1) // n + 1
    branch = jnp.clip((used + 2 * CHUNKS - 1) // (2 * CHUNKS) - 1, 0, len(lives) - 1)
    return lax.switch(branch, [functools.partial(solve, live) for live in lives])


def solution(mesh, nx=NX):
    placed = (
        P(None, "row", None, "col"),
        P(("col", "row"), None),
        P(("col", "row"), None, None),
        P(),
    )
    return jax.shard_map(
        functools.partial(body, nx),
        mesh=mesh,
        in_specs=placed,
        out_specs=(P(("col", "row"), None, None), P(("col", "row"), None, None)),
        check_vma=False,
    )
```

```python
import functools

import jax
import jax.numpy as jnp
from jax import lax
from jax.experimental import pallas as pl
from jax.experimental.pallas import tpu as pltpu
from jax.sharding import PartitionSpec as P

ITERS = 3
NX = 4
CHUNKS = 4
ROWS = 32
MESH = pl.DeviceIdType.MESH
F32 = jnp.float32
BF16 = jnp.bfloat16
LANES = 128
HALF = 64
CELLS = 16


def column_sums(values):
    total = jnp.sum(jnp.sum(values, axis=0), axis=0, keepdims=True)
    return total + pltpu.roll(total, HALF, 1)


def kernel(
    nx, nz, live,
    first_ref, matrix_hbm, diag_ref, right_ref,
    sol_ref, res_ref,
    raw, matrix, gathered, mirror, got_x, sums_z, got_z, first_z, sums_x, last_x,
    diagonal, direction, image, solution, residual_ref, slab_dir, slab_img,
    out1, in1, out2, in2, out_a, in_a, out_b, in_b, out_s, in_s,
    load_sem, gz_send, gz_recv, gx_send, gx_recv,
    mx_send, mx_recv, mz_send, mz_recv, fz_send, fz_recv, lx_send, lx_recv, hop_send, hop_recv,
):
    n = nx * nz
    pairs = diagonal.shape[0]
    order = n * CELLS
    block_rows = raw.shape[0]
    stored = raw.shape[2]
    per_chunk = live // CHUNKS
    turn_rows = min(ROWS, order)
    i = lax.axis_index("row")
    j = lax.axis_index("col")
    z = i // nx
    x = i % nx
    first = first_ref[0]
    my_row = (j - first) & (n - 1)
    my_block = (first + my_row) // n
    shift = first & (n - 1)
    odd = (my_block & 1) == 1

    barrier = pltpu.get_barrier_semaphore()

    def greet(step, c):
        for device in (((i + step) % n, j), (i, (j + step) % n)):
            pl.semaphore_signal(barrier, inc=1, device_id=device, device_id_type=MESH)
        return c

    lax.fori_loop(1, n, greet, 0)

    def load(a):
        return pltpu.make_async_copy(
            matrix_hbm.at[a, :, pl.ds(0, stored)], raw.at[a], load_sem.at[a]
        )

    for a in range(block_rows):
        load(a).start()

    block_of = (
        2 * lax.broadcasted_iota(jnp.int32, (pairs, CELLS, LANES), 0)
        + lax.broadcasted_iota(jnp.int32, (pairs, CELLS, LANES), 2) // HALF
    )
    owned = (block_of == my_block) | (block_of == my_block + 1)
    left_half = lax.broadcasted_iota(jnp.int32, (order, LANES), 1) < HALF
    even_lanes = (lax.broadcasted_iota(jnp.int32, (CELLS, LANES), 1) < HALF).astype(F32)
    even_mask = even_lanes.astype(BF16)
    odd_mask = (1.0 - even_lanes).astype(BF16)

    def swap(piece):
        return jnp.where(odd, pltpu.roll(piece, HALF, 1), piece)

    def rotated(slots, back):
        slots = slots.astype(F32)
        step = 1
        while step < n:
            cut = n - step if back else step
            moved = jnp.concatenate([slots[cut:], slots[:cut]], axis=0)
            slots = jnp.where((shift & step) != 0, moved, slots)
            step *= 2
        return slots.astype(BF16)

    def row_copy(src, dst, send, recv, zz, xx):
        return pltpu.make_async_remote_copy(
            src_ref=src, dst_ref=dst, send_sem=send, recv_sem=recv,
            device_id=(zz * nx + xx, j), device_id_type=MESH,
        )

    def hop_copy(src, dst, k, h, row, col):
        return pltpu.make_async_remote_copy(
            src_ref=src, dst_ref=dst, send_sem=hop_send.at[k, h],
            recv_sem=hop_recv.at[k, h], device_id=(row, col), device_id_type=MESH,
        )

    def hop_wait(buf, k, h, slots):
        part = buf.at[pl.ds(0, slots)]
        hop_copy(part, part, k, h, i, j).wait()

    def line_start(src, dst, k, h, target):
        def send(step, c):
            row, col = target(step)
            hop_copy(src(row, col), dst, k, h, row, col).start()
            return c

        lax.fori_loop(1, n, send, 0)

    def along_col(step):
        return i, (j + step) % n

    def along_row(step):
        return (i + step) % n, j

    def sums_start(k, h, value, along):
        out_s[k, h] = value
        place = j if along is along_col else i
        in_s[k, h, place] = value
        line_start(lambda r, c: out_s.at[k, h], in_s.at[k, h, place], k, 4 + h, along)

    def sums_end(k, h):
        hop_wait(in_s.at[k, h], k, 4 + h, n - 1)
        return jnp.sum(in_s[k, h], axis=0)

    def spread_z(k, dz):
        return row_copy(
            gathered.at[k, z, x], gathered.at[k, z, x],
            gz_send.at[k, dz - 1], gz_recv.at[k, dz - 1], (z + dz) % nz, x,
        )

    def spread_x(k, dx, dz):
        zz = (z - dz + nz) % nz
        return row_copy(
            gathered.at[k, zz, x], gathered.at[k, zz, x],
            gx_send.at[k, dz, dx - 1], gx_recv.at[k, dz, dx - 1], z, (x + dx) % nx,
        )

    def forward_z(k, dz):
        spread_z(k, dz).wait()
        for dx in range(1, nx):
            spread_x(k, dx, dz).start()

    def start(k, residual):
        out1[k] = swap(jnp.sum(jnp.where(owned, residual, 0.0), axis=0)).astype(BF16)
        in1[k, j] = out1[k]
        line_start(lambda r, c: out1.at[k], in1.at[k, j], k, 0, along_col)
        gathered[k, z, x] = residual[0:live].astype(BF16)
        for dz in range(1, nz):
            spread_z(k, dz).start()
        for dx in range(1, nx):
            spread_x(k, dx, 0).start()
        sums_start(k, 0, column_sums(residual * residual), along_col)

    for tile in range(2 * pairs // 8):
        values = jnp.swapaxes(right_ref[:, tile * 8 : tile * 8 + 8, :], 0, 1)
        for u in range(4):
            at = tile * 4 + u
            residual_ref[at] = jnp.concatenate([values[2 * u], values[2 * u + 1]], axis=1)
            diagonal[at] = jnp.concatenate(
                [
                    jnp.broadcast_to(diag_ref[:, 2 * at + h : 2 * at + h + 1], (CELLS, HALF))
                    for h in range(2)
                ],
                axis=1,
            )
    solution[...] = jnp.zeros_like(solution)
    direction[...] = jnp.zeros_like(direction)
    image[...] = jnp.zeros_like(image)
    slab_dir[...] = jnp.zeros_like(slab_dir)
    slab_img[...] = jnp.zeros_like(slab_img)
    pl.semaphore_wait(barrier, 2 * (n - 1))
    start(0, residual_ref[...])

    for a in range(block_rows):
        load(a).wait()
        slab_row = first + a * n + i

        def turn(q, c, a=a, slab_row=slab_row):
            at = pl.ds(pl.multiple_of(q * turn_rows, turn_rows), turn_rows)
            to = pl.ds(pl.multiple_of(a * order + q * turn_rows, turn_rows), turn_rows)
            for tile in range(live // 4):
                values = jnp.swapaxes(raw[a, at, tile * 8 : tile * 8 + 8, :], 0, 1)
                for b in range(8):
                    column = (tile * 8 + b) * n + j
                    weight = jnp.where(
                        column < slab_row, 1.0, jnp.where(column == slab_row, 0.5, 0.0)
                    )
                    matrix[tile * 8 + b, to] = values[b] * weight.astype(BF16)
            return c

        lax.fori_loop(0, order // turn_rows, turn, 0)

    def iteration(k, norm_old):
        residual = residual_ref[...]
        forward_z(k, 1)
        if nz > 2:
            forward_z(k, nz - 1)
        hop_wait(in1.at[k], k, 0, n - 1)
        out2[k] = rotated(in1[k], False)
        in2[k, i] = out2[k, i]
        line_start(lambda r, c: out2.at[k, r], in2.at[k, i], k, 1, along_row)
        for dz in range(2, nz - 1):
            forward_z(k, dz)
        sums_start(k, 1, sums_end(k, 0), along_row)
        hop_wait(in2.at[k], k, 1, n - 1)
        slab = in2[k].astype(F32).reshape(order, LANES)

        turned = jnp.transpose(slab).astype(BF16)
        both = jnp.concatenate([turned[0:HALF], turned[HALF:LANES]], axis=1)

        def mirror_x(chunk, dx):
            xx = (x + dx) % nx
            return row_copy(
                mirror.at[chunk, :, xx], got_x.at[k, chunk, dx - 1],
                mx_send.at[k, chunk, dx - 1], mx_recv.at[k, chunk, dx - 1], z, xx,
            )

        def mirror_z(chunk, dz):
            zz = (z + dz) % nz
            return row_copy(
                sums_z.at[chunk, zz], got_z.at[k, chunk, dz - 1],
                mz_send.at[k, chunk, dz - 1], mz_recv.at[k, chunk, dz - 1], zz, x,
            )

        def early_z(dz):
            zz = (z + dz) % nz
            return row_copy(
                mirror.at[0, zz], first_z.at[k, dz - 1],
                fz_send.at[k, dz - 1], fz_recv.at[k, dz - 1], zz, x,
            )

        def late_x(dx):
            xx = (x + dx) % nx
            return row_copy(
                sums_x.at[xx], last_x.at[k, dx - 1],
                lx_send.at[k, dx - 1], lx_recv.at[k, dx - 1], z, xx,
            )

        def pass_x():
            for dz in range(1, nz):
                early_z(dz).wait()
            for xx in range(nx):
                total = mirror[0, z, xx].astype(F32)
                for dz in range(1, nz):
                    total = total + first_z[k, dz - 1, xx].astype(F32)
                sums_x[xx] = total.astype(BF16)
            for dx in range(1, nx):
                late_x(dx).start()

        def transposed(chunk):
            for u in range(per_chunk):
                p = chunk * per_chunk + u
                parts = [
                    jnp.dot(both, matrix[2 * p + h], preferred_element_type=F32)
                    for h in range(2)
                ]
                cells = jnp.transpose(jnp.concatenate(parts, axis=0))
                mirror[chunk, :, :, u] = cells.astype(BF16).reshape(nz, nx, CELLS, LANES)

        def transposed_x(chunk, c):
            transposed(chunk)
            for dx in range(1, nx):
                mirror_x(chunk, dx).start()
            return c

        transposed(0)
        for dz in range(1, nz):
            early_z(dz).start()
        lax.fori_loop(1, CHUNKS, transposed_x, 0)

        def pass_z(chunk, c):
            for dx in range(1, nx):
                mirror_x(chunk, dx).wait()
            for dz in range(nz):
                zz = (z + dz) % nz
                total = mirror[chunk, zz, x].astype(F32)
                for dx in range(1, nx):
                    total = total + got_x[k, chunk, dx - 1, zz].astype(F32)
                sums_z[chunk, zz] = total.astype(BF16)
            for dz in range(1, nz):
                mirror_z(chunk, dz).start()
            return c

        norm = sums_end(k, 1)
        beta = jnp.where(k == 0, 0.0, norm / norm_old)
        slab_d = slab + beta * slab_dir[...]
        slab_dir[...] = slab_d
        beta_cell = beta.reshape(1, 1, LANES)
        cells_d = residual + beta_cell * direction[...]
        direction[...] = cells_d
        curve = column_sums(diagonal[...] * cells_d * cells_d)

        for dz in range(nz):
            for dx in range(1, nx):
                spread_x(k, dx, dz).wait()
        rows = None
        for half in range(2):
            left, right = [], []
            for u in range(live // 2):
                p = half * (live // 2) + u
                cells = gathered[k, :, :, p].reshape(n, CELLS, LANES)
                left += [matrix[2 * p], matrix[2 * p + 1]]
                right += [
                    (cells * even_mask).reshape(order, LANES),
                    (cells * odd_mask).reshape(order, LANES),
                ]
            part = jnp.dot(
                jnp.concatenate(left, axis=1),
                jnp.concatenate(right, axis=0),
                preferred_element_type=F32,
            )
            rows = part if rows is None else rows + part
        rows = rows + pltpu.roll(rows, HALF, 1)
        rows = jnp.where(left_half, rows[0:order], rows[order:])

        out_a[k] = rows.astype(BF16).reshape(n, CELLS, LANES)
        in_a[k, i] = out_a[k, i]
        line_start(lambda r, c: out_a.at[k, r], in_a.at[k, i], k, 2, along_row)
        slab_q = rows + beta * slab_img[...]
        slab_img[...] = slab_q
        curve = curve + 2.0 * column_sums((slab_d * slab_q).reshape(n, CELLS, LANES))
        sums_start(k, 2, curve, along_row)

        pass_x()
        pass_z(1, 0)
        pass_z(2, 0)

        hop_wait(in_a.at[k], k, 2, n - 1)
        out_b[k] = rotated(in_a[k], True)
        in_b[k, j] = out_b[k, j]
        line_start(lambda r, c: out_b.at[k, c], in_b.at[k, j], k, 3, along_col)
        sums_start(k, 3, sums_end(k, 2), along_col)
        pass_z(3, 0)

        def finish_z(chunk, c):
            for dz in range(1, nz):
                mirror_z(chunk, dz).wait()
            at = pl.ds(chunk * per_chunk, per_chunk)
            total = sums_z[chunk, z].astype(F32)
            for dz in range(1, nz):
                total = total + got_z[k, chunk, dz - 1].astype(F32)
            image[at] = image[at] + total
            return c

        image[...] = beta_cell * image[...] + diagonal[...] * residual
        lax.fori_loop(1, CHUNKS, finish_z, 0)
        for dx in range(1, nx):
            late_x(dx).wait()
        total = sums_x[x].astype(F32)
        for dx in range(1, nx):
            total = total + last_x[k, dx - 1].astype(F32)
        image[0:per_chunk] = image[0:per_chunk] + total
        applied = image[...]

        hop_wait(in_b.at[k], k, 3, n - 1)
        piece = swap(jnp.sum(in_b[k].astype(F32), axis=0))
        applied = applied + jnp.where(owned, piece.reshape(1, CELLS, LANES), 0.0)
        image[...] = applied
        length = (norm / sums_end(k, 3)).reshape(1, 1, LANES)
        residual = residual - length * applied
        residual_ref[...] = residual

        @pl.when(k < ITERS - 1)
        def _():
            start(k + 1, residual)

        solution[...] = solution[...] + length * cells_d
        return norm

    lax.fori_loop(0, ITERS, iteration, jnp.ones((1, LANES), F32))
    for source, target in ((solution, sol_ref), (residual_ref, res_ref)):
        for tile in range(2 * pairs // 8):
            halves = []
            for u in range(4):
                values = source[tile * 4 + u]
                halves += [values[:, 0:HALF], values[:, HALF:LANES]]
            target[:, tile * 8 : tile * 8 + 8, :] = jnp.swapaxes(jnp.stack(halves), 0, 1)


def body(nx, matrix, diagonal, right_side, slab_first):
    n = lax.axis_size("row")
    nz = n // nx
    rb, order, blocks, _ = matrix.shape
    cells = right_side.shape[0]
    pairs = blocks // 2
    vec = (pairs, cells, LANES)
    piece = (cells, LANES)
    vmem = pl.BlockSpec(memory_space=pltpu.VMEM)
    dma = pltpu.SemaphoreType.DMA

    def solve(live):
        stored = min(blocks, -(-2 * live // 16) * 16)
        shard = (live, cells, LANES)
        part = (live // CHUNKS, cells, LANES)
        return pl.pallas_call(
            functools.partial(kernel, nx, nz, live),
            out_shape=[jax.ShapeDtypeStruct(right_side.shape, F32)] * 2,
            in_specs=[
                pl.BlockSpec(memory_space=pltpu.SMEM),
                pl.BlockSpec(memory_space=pl.ANY),
                vmem,
                vmem,
            ],
            out_specs=[vmem, vmem],
            scratch_shapes=[
                pltpu.VMEM((rb, order, stored, order), BF16),
                pltpu.VMEM((2 * live, rb * order, order), BF16),
                pltpu.VMEM((ITERS, nz, nx) + shard, BF16),
                pltpu.VMEM((CHUNKS, nz, nx) + part, BF16),
                pltpu.VMEM((ITERS, CHUNKS, nx - 1, nz) + part, BF16),
                pltpu.VMEM((CHUNKS, nz) + part, BF16),
                pltpu.VMEM((ITERS, CHUNKS, nz - 1) + part, BF16),
                pltpu.VMEM((ITERS, nz - 1, nx) + part, BF16),
                pltpu.VMEM((nx,) + part, BF16),
                pltpu.VMEM((ITERS, nx - 1) + part, BF16),
                pltpu.VMEM(vec, F32),
                pltpu.VMEM(vec, F32),
                pltpu.VMEM(vec, F32),
                pltpu.VMEM(vec, F32),
                pltpu.VMEM(vec, F32),
                pltpu.VMEM((order, LANES), F32),
                pltpu.VMEM((order, LANES), F32),
                pltpu.VMEM((ITERS,) + piece, BF16),
                pltpu.VMEM((ITERS, n) + piece, BF16),
                pltpu.VMEM((ITERS, n) + piece, BF16),
                pltpu.VMEM((ITERS, n) + piece, BF16),
                pltpu.VMEM((ITERS, n) + piece, BF16),
                pltpu.VMEM((ITERS, n) + piece, BF16),
                pltpu.VMEM((ITERS, n) + piece, BF16),
                pltpu.VMEM((ITERS, n) + piece, BF16),
                pltpu.VMEM((ITERS, 4, 1, LANES), F32),
                pltpu.VMEM((ITERS, 4, n, 1, LANES), F32),
                dma((rb,)),
                dma((ITERS, nz - 1)),
                dma((ITERS, nz - 1)),
                dma((ITERS, nz, nx - 1)),
                dma((ITERS, nz, nx - 1)),
                dma((ITERS, CHUNKS, nx - 1)),
                dma((ITERS, CHUNKS, nx - 1)),
                dma((ITERS, CHUNKS, nz - 1)),
                dma((ITERS, CHUNKS, nz - 1)),
                dma((ITERS, nz - 1)),
                dma((ITERS, nz - 1)),
                dma((ITERS, nx - 1)),
                dma((ITERS, nx - 1)),
                dma((ITERS, 8)),
                dma((ITERS, 8)),
            ],
            compiler_params=pltpu.CompilerParams(
                collective_id=live // CHUNKS,
                has_side_effects=True,
                vmem_limit_bytes=56 * 1024 * 1024,
            ),
            name=f"conjugate_gradients_{live}",
        )(slab_first, matrix, diagonal, right_side)

    lives = range(CHUNKS, pairs + 1, CHUNKS)
    used = (slab_first[0] + rb * n - 1) // n + 1
    branch = jnp.clip((used + 2 * CHUNKS - 1) // (2 * CHUNKS) - 1, 0, len(lives) - 1)
    return lax.switch(branch, [functools.partial(solve, live) for live in lives])


def solution(mesh, nx=NX):
    placed = (
        P(None, "row", None, "col"),
        P(("col", "row"), None),
        P(("col", "row"), None, None),
        P(),
    )
    return jax.shard_map(
        functools.partial(body, nx),
        mesh=mesh,
        in_specs=placed,
        out_specs=(P(("col", "row"), None, None), P(("col", "row"), None, None)),
        check_vma=False,
    )
```

```python
import functools

import jax
import jax.numpy as jnp
from jax import lax
from jax.experimental import pallas as pl
from jax.experimental.pallas import tpu as pltpu
from jax.sharding import PartitionSpec as P

ITERS = 3
NX = 4
CHUNKS = 4
ROWS = 32
MESH = pl.DeviceIdType.MESH
F32 = jnp.float32
BF16 = jnp.bfloat16
LANES = 128
HALF = 64
CELLS = 16


def column_sums(values):
    total = jnp.sum(jnp.sum(values, axis=0), axis=0, keepdims=True)
    return total + pltpu.roll(total, HALF, 1)


def kernel(
    nx, nz, live,
    first_ref, matrix_hbm, diag_ref, right_ref,
    sol_ref, res_ref,
    raw, matrix, gathered, mirror, got_x, sums_z, got_z, first_z, sums_x, last_x,
    diagonal, direction, image, solution, residual_ref, slab_dir, slab_img,
    out1, in1, out2, in2, out_a, in_a, out_b, in_b, out_s, in_s,
    load_sem, gz_send, gz_recv, gx_send, gx_recv,
    mx_send, mx_recv, mz_send, mz_recv, fz_send, fz_recv, lx_send, lx_recv, hop_send, hop_recv,
):
    n = nx * nz
    pairs = diagonal.shape[0]
    order = n * CELLS
    block_rows = raw.shape[0]
    stored = raw.shape[2]
    per_chunk = live // CHUNKS
    turn_rows = min(ROWS, order)
    i = lax.axis_index("row")
    j = lax.axis_index("col")
    z = i // nx
    x = i % nx
    first = first_ref[0]
    my_row = (j - first) & (n - 1)
    my_block = (first + my_row) // n
    shift = first & (n - 1)
    odd = (my_block & 1) == 1

    barrier = pltpu.get_barrier_semaphore()

    def greet(step, c):
        for device in (((i + step) % n, j), (i, (j + step) % n)):
            pl.semaphore_signal(barrier, inc=1, device_id=device, device_id_type=MESH)
        return c

    lax.fori_loop(1, n, greet, 0)

    def load(a):
        return pltpu.make_async_copy(
            matrix_hbm.at[a, :, pl.ds(0, stored)], raw.at[a], load_sem.at[a]
        )

    for a in range(block_rows):
        load(a).start()

    block_of = (
        2 * lax.broadcasted_iota(jnp.int32, (pairs, CELLS, LANES), 0)
        + lax.broadcasted_iota(jnp.int32, (pairs, CELLS, LANES), 2) // HALF
    )
    owned = (block_of == my_block) | (block_of == my_block + 1)
    left_half = lax.broadcasted_iota(jnp.int32, (order, LANES), 1) < HALF
    even_lanes = (lax.broadcasted_iota(jnp.int32, (CELLS, LANES), 1) < HALF).astype(F32)
    even_mask = even_lanes.astype(BF16)
    odd_mask = (1.0 - even_lanes).astype(BF16)

    def swap(piece):
        return jnp.where(odd, pltpu.roll(piece, HALF, 1), piece)

    def rotated(slots, back):
        slots = slots.astype(F32)
        step = 1
        while step < n:
            cut = n - step if back else step
            moved = jnp.concatenate([slots[cut:], slots[:cut]], axis=0)
            slots = jnp.where((shift & step) != 0, moved, slots)
            step *= 2
        return slots.astype(BF16)

    def row_copy(src, dst, send, recv, zz, xx):
        return pltpu.make_async_remote_copy(
            src_ref=src, dst_ref=dst, send_sem=send, recv_sem=recv,
            device_id=(zz * nx + xx, j), device_id_type=MESH,
        )

    def hop_copy(src, dst, k, h, row, col):
        return pltpu.make_async_remote_copy(
            src_ref=src, dst_ref=dst, send_sem=hop_send.at[k, h],
            recv_sem=hop_recv.at[k, h], device_id=(row, col), device_id_type=MESH,
        )

    def hop_wait(buf, k, h, slots):
        part = buf.at[pl.ds(0, slots)]
        hop_copy(part, part, k, h, i, j).wait()

    def line_start(src, dst, k, h, target):
        def send(step, c):
            row, col = target(step)
            hop_copy(src(row, col), dst, k, h, row, col).start()
            return c

        lax.fori_loop(1, n, send, 0)

    def along_col(step):
        return i, (j + step) % n

    def along_row(step):
        return (i + step) % n, j

    def sums_start(k, h, value, along):
        out_s[k, h] = value
        place = j if along is along_col else i
        in_s[k, h, place] = value
        line_start(lambda r, c: out_s.at[k, h], in_s.at[k, h, place], k, 4 + h, along)

    def sums_end(k, h):
        hop_wait(in_s.at[k, h], k, 4 + h, n - 1)
        return jnp.sum(in_s[k, h], axis=0)

    def spread_z(k, dz):
        return row_copy(
            gathered.at[k, z, x], gathered.at[k, z, x],
            gz_send.at[k, dz - 1], gz_recv.at[k, dz - 1], (z + dz) % nz, x,
        )

    def spread_x(k, dx, dz):
        zz = (z - dz + nz) % nz
        return row_copy(
            gathered.at[k, zz, x], gathered.at[k, zz, x],
            gx_send.at[k, dz, dx - 1], gx_recv.at[k, dz, dx - 1], z, (x + dx) % nx,
        )

    def forward_z(k, dz):
        spread_z(k, dz).wait()
        for dx in range(1, nx):
            spread_x(k, dx, dz).start()

    def start(k, residual):
        out1[k] = swap(jnp.sum(jnp.where(owned, residual, 0.0), axis=0)).astype(BF16)
        in1[k, j] = out1[k]
        line_start(lambda r, c: out1.at[k], in1.at[k, j], k, 0, along_col)
        gathered[k, z, x] = residual[0:live].astype(BF16)
        for dz in range(1, nz):
            spread_z(k, dz).start()
        for dx in range(1, nx):
            spread_x(k, dx, 0).start()
        sums_start(k, 0, column_sums(residual * residual), along_col)

    for tile in range(2 * pairs // 8):
        values = jnp.swapaxes(right_ref[:, tile * 8 : tile * 8 + 8, :], 0, 1)
        for u in range(4):
            at = tile * 4 + u
            residual_ref[at] = jnp.concatenate([values[2 * u], values[2 * u + 1]], axis=1)
            diagonal[at] = jnp.concatenate(
                [
                    jnp.broadcast_to(diag_ref[:, 2 * at + h : 2 * at + h + 1], (CELLS, HALF))
                    for h in range(2)
                ],
                axis=1,
            )
    solution[...] = jnp.zeros_like(solution)
    direction[...] = jnp.zeros_like(direction)
    image[...] = jnp.zeros_like(image)
    slab_dir[...] = jnp.zeros_like(slab_dir)
    slab_img[...] = jnp.zeros_like(slab_img)
    pl.semaphore_wait(barrier, 2 * (n - 1))
    start(0, residual_ref[...])

    for a in range(block_rows):
        load(a).wait()
        slab_row = first + a * n + i

        def turn(q, c, a=a, slab_row=slab_row):
            at = pl.ds(pl.multiple_of(q * turn_rows, turn_rows), turn_rows)
            to = pl.ds(pl.multiple_of(a * order + q * turn_rows, turn_rows), turn_rows)
            for tile in range(live // 4):
                values = jnp.swapaxes(raw[a, at, tile * 8 : tile * 8 + 8, :], 0, 1)
                for b in range(8):
                    column = (tile * 8 + b) * n + j
                    weight = jnp.where(
                        column < slab_row, 1.0, jnp.where(column == slab_row, 0.5, 0.0)
                    )
                    matrix[tile * 8 + b, to] = values[b] * weight.astype(BF16)
            return c

        lax.fori_loop(0, order // turn_rows, turn, 0)

    def iteration(k, norm_old):
        residual = residual_ref[...]
        forward_z(k, 1)
        if nz > 2:
            forward_z(k, nz - 1)
        hop_wait(in1.at[k], k, 0, n - 1)
        out2[k] = rotated(in1[k], False)
        in2[k, i] = out2[k, i]
        line_start(lambda r, c: out2.at[k, r], in2.at[k, i], k, 1, along_row)
        for dz in range(2, nz - 1):
            forward_z(k, dz)
        sums_start(k, 1, sums_end(k, 0), along_row)
        hop_wait(in2.at[k], k, 1, n - 1)
        slab = in2[k].astype(F32).reshape(order, LANES)

        turned = jnp.transpose(slab).astype(BF16)
        both = jnp.concatenate([turned[0:HALF], turned[HALF:LANES]], axis=1)

        def mirror_x(chunk, dx):
            xx = (x + dx) % nx
            return row_copy(
                mirror.at[chunk, :, xx], got_x.at[k, chunk, dx - 1],
                mx_send.at[k, chunk, dx - 1], mx_recv.at[k, chunk, dx - 1], z, xx,
            )

        def mirror_z(chunk, dz):
            zz = (z + dz) % nz
            return row_copy(
                sums_z.at[chunk, zz], got_z.at[k, chunk, dz - 1],
                mz_send.at[k, chunk, dz - 1], mz_recv.at[k, chunk, dz - 1], zz, x,
            )

        def early_z(dz):
            zz = (z + dz) % nz
            return row_copy(
                mirror.at[0, zz], first_z.at[k, dz - 1],
                fz_send.at[k, dz - 1], fz_recv.at[k, dz - 1], zz, x,
            )

        def late_x(dx):
            xx = (x + dx) % nx
            return row_copy(
                sums_x.at[xx], last_x.at[k, dx - 1],
                lx_send.at[k, dx - 1], lx_recv.at[k, dx - 1], z, xx,
            )

        def pass_x():
            for dz in range(1, nz):
                early_z(dz).wait()
            for xx in range(nx):
                total = mirror[0, z, xx].astype(F32)
                for dz in range(1, nz):
                    total = total + first_z[k, dz - 1, xx].astype(F32)
                sums_x[xx] = total.astype(BF16)
            for dx in range(1, nx):
                late_x(dx).start()

        def transposed(chunk):
            for u in range(per_chunk):
                p = chunk * per_chunk + u
                parts = [
                    jnp.dot(both, matrix[2 * p + h], preferred_element_type=F32)
                    for h in range(2)
                ]
                cells = jnp.transpose(jnp.concatenate(parts, axis=0))
                mirror[chunk, :, :, u] = cells.astype(BF16).reshape(nz, nx, CELLS, LANES)

        def transposed_x(chunk, c):
            transposed(chunk)
            for dx in range(1, nx):
                mirror_x(chunk, dx).start()
            return c

        transposed(0)
        for dz in range(1, nz):
            early_z(dz).start()
        lax.fori_loop(1, CHUNKS, transposed_x, 0)

        def pass_z(chunk, c):
            for dx in range(1, nx):
                mirror_x(chunk, dx).wait()
            for dz in range(nz):
                zz = (z + dz) % nz
                total = mirror[chunk, zz, x].astype(F32)
                for dx in range(1, nx):
                    total = total + got_x[k, chunk, dx - 1, zz].astype(F32)
                sums_z[chunk, zz] = total.astype(BF16)
            for dz in range(1, nz):
                mirror_z(chunk, dz).start()
            return c

        norm = sums_end(k, 1)
        beta = jnp.where(k == 0, 0.0, norm / norm_old)
        slab_d = slab + beta * slab_dir[...]
        slab_dir[...] = slab_d
        beta_cell = beta.reshape(1, 1, LANES)
        cells_d = residual + beta_cell * direction[...]
        direction[...] = cells_d
        curve = column_sums(diagonal[...] * cells_d * cells_d)

        for dz in range(nz):
            for dx in range(1, nx):
                spread_x(k, dx, dz).wait()
        rows = None
        for half in range(2):
            left, right = [], []
            for u in range(live // 2):
                p = half * (live // 2) + u
                cells = gathered[k, :, :, p].reshape(n, CELLS, LANES)
                left += [matrix[2 * p], matrix[2 * p + 1]]
                right += [
                    (cells * even_mask).reshape(order, LANES),
                    (cells * odd_mask).reshape(order, LANES),
                ]
            part = jnp.dot(
                jnp.concatenate(left, axis=1),
                jnp.concatenate(right, axis=0),
                preferred_element_type=F32,
            )
            rows = part if rows is None else rows + part
        rows = rows + pltpu.roll(rows, HALF, 1)
        rows = jnp.where(left_half, rows[0:order], rows[order:])

        out_a[k] = rows.astype(BF16).reshape(n, CELLS, LANES)
        in_a[k, i] = out_a[k, i]
        line_start(lambda r, c: out_a.at[k, r], in_a.at[k, i], k, 2, along_row)
        slab_q = rows + beta * slab_img[...]
        slab_img[...] = slab_q
        curve = curve + 2.0 * column_sums((slab_d * slab_q).reshape(n, CELLS, LANES))
        sums_start(k, 2, curve, along_row)

        pass_x()
        pass_z(1, 0)

        hop_wait(in_a.at[k], k, 2, n - 1)
        out_b[k] = rotated(in_a[k], True)
        in_b[k, j] = out_b[k, j]
        line_start(lambda r, c: out_b.at[k, c], in_b.at[k, j], k, 3, along_col)
        sums_start(k, 3, sums_end(k, 2), along_col)
        pass_z(2, 0)
        pass_z(3, 0)

        def finish_z(chunk, c):
            for dz in range(1, nz):
                mirror_z(chunk, dz).wait()
            at = pl.ds(chunk * per_chunk, per_chunk)
            total = sums_z[chunk, z].astype(F32)
            for dz in range(1, nz):
                total = total + got_z[k, chunk, dz - 1].astype(F32)
            image[at] = image[at] + total
            return c

        image[...] = beta_cell * image[...] + diagonal[...] * residual
        lax.fori_loop(1, CHUNKS, finish_z, 0)
        for dx in range(1, nx):
            late_x(dx).wait()
        total = sums_x[x].astype(F32)
        for dx in range(1, nx):
            total = total + last_x[k, dx - 1].astype(F32)
        image[0:per_chunk] = image[0:per_chunk] + total
        applied = image[...]

        hop_wait(in_b.at[k], k, 3, n - 1)
        piece = swap(jnp.sum(in_b[k].astype(F32), axis=0))
        applied = applied + jnp.where(owned, piece.reshape(1, CELLS, LANES), 0.0)
        image[...] = applied
        length = (norm / sums_end(k, 3)).reshape(1, 1, LANES)
        residual = residual - length * applied
        residual_ref[...] = residual

        @pl.when(k < ITERS - 1)
        def _():
            start(k + 1, residual)

        solution[...] = solution[...] + length * cells_d
        return norm

    lax.fori_loop(0, ITERS, iteration, jnp.ones((1, LANES), F32))
    for source, target in ((solution, sol_ref), (residual_ref, res_ref)):
        for tile in range(2 * pairs // 8):
            halves = []
            for u in range(4):
                values = source[tile * 4 + u]
                halves += [values[:, 0:HALF], values[:, HALF:LANES]]
            target[:, tile * 8 : tile * 8 + 8, :] = jnp.swapaxes(jnp.stack(halves), 0, 1)


def body(nx, matrix, diagonal, right_side, slab_first):
    n = lax.axis_size("row")
    nz = n // nx
    rb, order, blocks, _ = matrix.shape
    cells = right_side.shape[0]
    pairs = blocks // 2
    vec = (pairs, cells, LANES)
    piece = (cells, LANES)
    vmem = pl.BlockSpec(memory_space=pltpu.VMEM)
    dma = pltpu.SemaphoreType.DMA

    def solve(live):
        stored = min(blocks, -(-2 * live // 16) * 16)
        shard = (live, cells, LANES)
        part = (live // CHUNKS, cells, LANES)
        return pl.pallas_call(
            functools.partial(kernel, nx, nz, live),
            out_shape=[jax.ShapeDtypeStruct(right_side.shape, F32)] * 2,
            in_specs=[
                pl.BlockSpec(memory_space=pltpu.SMEM),
                pl.BlockSpec(memory_space=pl.ANY),
                vmem,
                vmem,
            ],
            out_specs=[vmem, vmem],
            scratch_shapes=[
                pltpu.VMEM((rb, order, stored, order), BF16),
                pltpu.VMEM((2 * live, rb * order, order), BF16),
                pltpu.VMEM((ITERS, nz, nx) + shard, BF16),
                pltpu.VMEM((CHUNKS, nz, nx) + part, BF16),
                pltpu.VMEM((ITERS, CHUNKS, nx - 1, nz) + part, BF16),
                pltpu.VMEM((CHUNKS, nz) + part, BF16),
                pltpu.VMEM((ITERS, CHUNKS, nz - 1) + part, BF16),
                pltpu.VMEM((ITERS, nz - 1, nx) + part, BF16),
                pltpu.VMEM((nx,) + part, BF16),
                pltpu.VMEM((ITERS, nx - 1) + part, BF16),
                pltpu.VMEM(vec, F32),
                pltpu.VMEM(vec, F32),
                pltpu.VMEM(vec, F32),
                pltpu.VMEM(vec, F32),
                pltpu.VMEM(vec, F32),
                pltpu.VMEM((order, LANES), F32),
                pltpu.VMEM((order, LANES), F32),
                pltpu.VMEM((ITERS,) + piece, BF16),
                pltpu.VMEM((ITERS, n) + piece, BF16),
                pltpu.VMEM((ITERS, n) + piece, BF16),
                pltpu.VMEM((ITERS, n) + piece, BF16),
                pltpu.VMEM((ITERS, n) + piece, BF16),
                pltpu.VMEM((ITERS, n) + piece, BF16),
                pltpu.VMEM((ITERS, n) + piece, BF16),
                pltpu.VMEM((ITERS, n) + piece, BF16),
                pltpu.VMEM((ITERS, 4, 1, LANES), F32),
                pltpu.VMEM((ITERS, 4, n, 1, LANES), F32),
                dma((rb,)),
                dma((ITERS, nz - 1)),
                dma((ITERS, nz - 1)),
                dma((ITERS, nz, nx - 1)),
                dma((ITERS, nz, nx - 1)),
                dma((ITERS, CHUNKS, nx - 1)),
                dma((ITERS, CHUNKS, nx - 1)),
                dma((ITERS, CHUNKS, nz - 1)),
                dma((ITERS, CHUNKS, nz - 1)),
                dma((ITERS, nz - 1)),
                dma((ITERS, nz - 1)),
                dma((ITERS, nx - 1)),
                dma((ITERS, nx - 1)),
                dma((ITERS, 8)),
                dma((ITERS, 8)),
            ],
            compiler_params=pltpu.CompilerParams(
                collective_id=live // CHUNKS,
                has_side_effects=True,
                vmem_limit_bytes=56 * 1024 * 1024,
            ),
            name=f"conjugate_gradients_{live}",
        )(slab_first, matrix, diagonal, right_side)

    lives = range(CHUNKS, pairs + 1, CHUNKS)
    used = (slab_first[0] + rb * n - 1) // n + 1
    branch = jnp.clip((used + 2 * CHUNKS - 1) // (2 * CHUNKS) - 1, 0, len(lives) - 1)
    return lax.switch(branch, [functools.partial(solve, live) for live in lives])


def solution(mesh, nx=NX):
    placed = (
        P(None, "row", None, "col"),
        P(("col", "row"), None),
        P(("col", "row"), None, None),
        P(),
    )
    return jax.shard_map(
        functools.partial(body, nx),
        mesh=mesh,
        in_specs=placed,
        out_specs=(P(("col", "row"), None, None), P(("col", "row"), None, None)),
        check_vma=False,
    )
```
